512 devices in a mesh: seq: 64 (over x_lo, z, core), head: 8 (over x_hi, y).
Axes of the slice: x: 4 (x_hi: 2, x_lo: 2; x = x_hi * 2 + x_lo), y: 4, z: 16, core: 2. Of those that a mesh axis runs over, the one named last changes fastest.
Arguments:
- query_in: bfloat16 [8192, 5120], P('seq', 'head'), may hold values from -8 to 8
- key_in: bfloat16 [8192, 5120], P('seq', 'head'), may hold values from -8 to 8
- value_in: bfloat16 [8192, 5120], P('seq', 'head'), may hold values from -6 to 6
- grad_out: bfloat16 [8192, 5120], P('seq', 'head'), may hold values from -6 to 6
- offsets: int32 [5, 40], P(None, 'head'), may hold values from 0 to 15, as said below
Outputs:
- attended: bfloat16 [8192, 5120], P('seq', 'head')
- log_norm: float32 [40, 8192], P('head', 'seq')
- grad_query: bfloat16 [8192, 5120], P('seq', 'head')
- grad_key: bfloat16 [8192, 5120], P('seq', 'head')
- grad_value: bfloat16 [8192, 5120], P('seq', 'head')
The draws below stay inside these ranges and needn't reach their ends.
Inputs may be any that keep to these rules, and one draw needn't show every extreme that they name: offsets[l, h] is below 2^l for level l counted from 0; at the last level some head has offset 2^(4) - 1.
All inputs are finite; a program needn't handle non-finite values.
Results may differ from the reference program's by a relative error of at most 0.034.
Values may be sent and summed in bfloat16 or wider, within the bound.
A program may use at most 128 MiB of HBM per device.

```python
from functools import reduce
import jax
import jax.numpy as jnp
from jax import lax

HEADS = 40
DH = 128
SUB = 512
SEQ = 8192
LEVELS = 5


def base_sample(key, salt_value):
    subkey = jax.random.fold_in(key, salt_value)
    return jnp.clip(jax.random.normal(subkey, (SEQ, HEADS * DH), jnp.float32), -6.0, 6.0)


def draw_query_in(key, part):
    sample = base_sample(key, 1)
    return sample.astype(jnp.bfloat16)


def draw_key_in(key, part):
    sample = base_sample(key, 2)
    return sample.astype(jnp.bfloat16)


def draw_offsets(key, part):
    level_key, head_key = jax.random.split(jax.random.fold_in(key, 7))
    limits = 2 ** jnp.arange(LEVELS, dtype=jnp.int32)
    offsets = jax.random.randint(level_key, (LEVELS, HEADS), 0, limits[:, None], dtype=jnp.int32)
    chosen = jax.random.randint(head_key, (), 0, HEADS, dtype=jnp.int32)
    return offsets.at[LEVELS - 1, chosen].set(limits[LEVELS - 1] - 1)


def block_levels(stream_key, dims, shards, smallest, high):
    factor_of = 1.0
    for dim, shards_of in shards:
        heights = jax.random.uniform(jax.random.fold_in(jax.random.fold_in(stream_key, 6), dim), (shards_of,), jnp.float32, smallest / len(shards), high / len(shards))
        factor_of = factor_of * jnp.repeat(jnp.exp(heights), dims[dim] // shards_of).reshape((-1,) + (1,) * (len(dims) - 1 - dim))
    return factor_of


def gaussian(rng, dims, scale, limit, shards=(), held_as=jnp.bfloat16):
    values = scale * jax.random.normal(rng, dims, jnp.float32)
    if shards:
        values = values * block_levels(rng, dims, shards, -0.22, 0.18)
    return jnp.clip(values, -limit, limit).astype(held_as)


def setup_inputs(seed: int = 0) -> dict:
    key_of = jax.random.split(jax.random.key(seed), 6)
    return {
        "query_in": draw_query_in(jax.random.fold_in(key_of[5], 71), 0),
        "key_in": draw_key_in(jax.random.fold_in(key_of[5], 71), 0),
        "value_in": gaussian(key_of[2], (SEQ, HEADS * DH), 1.0, 6.0, ((0, 64), (1, 8))),
        "grad_out": gaussian(key_of[3], (SEQ, HEADS * DH), 1.0, 6.0, ((0, 64), (1, 8))),
        "offsets": draw_offsets(jax.random.fold_in(key_of[5], 71), 0),
    }


masked_score = -1e30


def rounded(source):
    return lax.optimization_barrier(source.astype(jnp.bfloat16)).astype(jnp.float32)


def select_rows(source, offset_row, dilation):
    row_count = source.shape[0] // dilation
    reshaped = source.reshape((row_count, dilation) + source.shape[1:])
    index_grid = offset_row.astype(jnp.int32).reshape((1, 1, offset_row.shape[0]) + (1,) * (source.ndim - 2))
    index_grid = jnp.broadcast_to(index_grid, (row_count, 1) + source.shape[1:])
    return jnp.take_along_axis(reshaped, index_grid, axis=1)[:, 0]


def spread_rows(source, offset_row, dilation, filler):
    row_count = source.shape[0]
    matches = jnp.arange(dilation, dtype=jnp.int32)[:, None] == offset_row.astype(jnp.int32)[None, :]
    matches = matches.reshape((1, dilation, offset_row.shape[0]) + (1,) * (source.ndim - 2))
    widened = jnp.where(matches, source[:, None], filler)
    return widened.reshape((row_count * dilation,) + source.shape[1:])


def reference(query_in, key_in, value_in, grad_out, offsets):
    score_scale = DH ** -0.5
    layout = (SEQ, HEADS, DH)
    queries = query_in.reshape(layout)
    keys_all = key_in.reshape(layout)
    values_all = value_in.reshape(layout)
    grads_all = grad_out.reshape(layout)
    causal = jnp.tril(jnp.ones((SUB, SUB), dtype=bool))

    def segment_scores(seg_query, seg_key):
        scores = jnp.einsum('qhd,khd->hqk', seg_query.astype(jnp.float32), seg_key.astype(jnp.float32)) * score_scale
        return jnp.where(causal[None], scores, masked_score)

    def forward_segment(inputs):
        seg_query, seg_key, seg_value = inputs
        scores = segment_scores(seg_query, seg_key)
        row_max = jnp.max(scores, axis=-1)
        weights = jnp.exp(scores - row_max[:, :, None])
        row_total = jnp.sum(weights, axis=-1)
        weighted = jnp.einsum('hqk,khd->qhd', rounded(weights), seg_value.astype(jnp.float32))
        return row_max.T, row_total.T, weighted

    pieces = []
    for level_id in range(LEVELS):
        dilation = 2 ** level_id
        offset_row = offsets[level_id]
        segments = SEQ // (SUB * dilation)
        level_parts = tuple(select_rows(source, offset_row, dilation).reshape(segments, SUB, HEADS, DH) for source in (queries, keys_all, values_all))
        row_max, row_total, weighted = lax.map(forward_segment, level_parts)
        row_count = SEQ // dilation
        pieces.append((row_max.reshape(row_count, HEADS), row_total.reshape(row_count, HEADS), weighted.reshape(row_count, HEADS, DH)))

    spread_max = [spread_rows(pieces[i][0], offsets[i], 2 ** i, masked_score) for i in range(LEVELS)]
    overall = reduce(jnp.maximum, spread_max)
    sum_total = jnp.zeros_like(overall)
    for i in range(LEVELS):
        sum_total = sum_total + spread_rows(pieces[i][1], offsets[i], 2 ** i, 0.0) * jnp.exp(spread_max[i] - overall)
    log_total = overall + jnp.log(sum_total)
    combined = jnp.zeros(layout, jnp.float32)
    for i in range(LEVELS):
        factor = jnp.exp(pieces[i][0] - select_rows(log_total, offsets[i], 2 ** i))
        combined = combined + spread_rows(pieces[i][2] * factor[:, :, None], offsets[i], 2 ** i, 0.0)
    out_values = rounded(combined)
    delta_rows = jnp.sum(grads_all.astype(jnp.float32) * out_values, axis=-1)

    def backward_segment(inputs):
        seg_query, seg_key, seg_value, seg_grad, seg_lse, seg_delta = inputs
        scores = segment_scores(seg_query, seg_key)
        probabilities = jnp.exp(scores - seg_lse.T[:, :, None])
        prob_grad = jnp.einsum('qhd,khd->hqk', seg_grad.astype(jnp.float32), seg_value.astype(jnp.float32))
        score_grad = rounded(score_scale * probabilities * (prob_grad - seg_delta.T[:, :, None]))
        query_part = jnp.einsum('hqk,khd->qhd', score_grad, seg_key.astype(jnp.float32))
        key_part = jnp.einsum('hqk,qhd->khd', score_grad, seg_query.astype(jnp.float32))
        value_part = jnp.einsum('hqk,qhd->khd', rounded(probabilities), seg_grad.astype(jnp.float32))
        return query_part, key_part, value_part

    query_grad = jnp.zeros(layout, jnp.float32)
    key_grad = jnp.zeros(layout, jnp.float32)
    value_grad = jnp.zeros(layout, jnp.float32)
    for level_id in range(LEVELS):
        dilation = 2 ** level_id
        offset_row = offsets[level_id]
        segments = SEQ // (SUB * dilation)
        level_parts = tuple(select_rows(source, offset_row, dilation).reshape(segments, SUB, HEADS, DH) for source in (queries, keys_all, values_all, grads_all))
        stat_parts = tuple(select_rows(source, offset_row, dilation).reshape(segments, SUB, HEADS) for source in (log_total, delta_rows))
        query_part, key_part, value_part = lax.map(backward_segment, level_parts + stat_parts)
        row_count = SEQ // dilation
        query_grad = query_grad + spread_rows(query_part.reshape(row_count, HEADS, DH), offset_row, dilation, 0.0)
        key_grad = key_grad + spread_rows(key_part.reshape(row_count, HEADS, DH), offset_row, dilation, 0.0)
        value_grad = value_grad + spread_rows(value_part.reshape(row_count, HEADS, DH), offset_row, dilation, 0.0)

    flat_shape = (SEQ, HEADS * DH)
    return (combined.astype(jnp.bfloat16).reshape(flat_shape), log_total.T,
            query_grad.astype(jnp.bfloat16).reshape(flat_shape),
            key_grad.astype(jnp.bfloat16).reshape(flat_shape),
            value_grad.astype(jnp.bfloat16).reshape(flat_shape))
```

```python
import jax
import jax.numpy as jnp
from jax import lax
from jax.experimental import pallas as pl
from jax.experimental.pallas import tpu as pltpu
from jax.sharding import PartitionSpec as P

MESH = pl.DeviceIdType.MESH
F32 = jnp.float32
BF16 = jnp.bfloat16

SEQ_DEVICES = 64
HEADS = 5
LEVELS = 5
DH = 128
TOKENS = 128
SUB = 512
HALF = 256
SCALE = DH ** (-0.5)
MASKED = -1e30

GROUP = [4 << level for level in range(LEVELS)]
ROWS = [TOKENS >> level for level in range(LEVELS)]
PLACE = [
    [0, 1, 2, 3, 0],
    [2, 3, 4, 5, 1],
    [5, 6, 7, 9, 10],
    [3, 11, 14, 18, 27],
    [1, 13, 17, 45, 49],
]
SLOT = [[0, 0, 0, 0, 2], [1] * 5, [2] * 5, [2] * 5, [2] * 5]
FIRST = [0, 0, 64, 96, 112]
TILE_BASE = [0, 4, 12]


def dot(a, b, dims, precision=None):
    return lax.dot_general(a, b, (dims, ((), ())), precision=precision, preferred_element_type=F32)


def nn(a, b):
    return dot(a, b, ((1,), (0,)))


def nt(a, b):
    return dot(a, b, ((1,), (1,)))


def tn(a, b):
    return dot(a, b, ((0,), (0,)))


def position(index, off_ref, head):
    return jnp.where(
        index < 64,
        2 * index + off_ref[1, head],
        jnp.where(
            index < 96,
            4 * (index - 64) + off_ref[2, head],
            jnp.where(
                index < 112,
                8 * (index - 96) + off_ref[3, head],
                16 * ((index - 112) & 7) + off_ref[4, head],
            ),
        ),
    )


def kernel(
    q_ref, k_ref, v_ref, g_ref, off_ref,
    out_ref, lse_ref, dq_ref, dk_ref, dv_ref,
    s0, sbuf, s4, ubuf, u4, ebuf, dbuf, abuf, stbuf, stin, cout, cin, obuf, o4, r0, rbuf, r4,
    in_send, in_recv, st_send, st_recv, c_send, c_recv, res_send, res_recv,
):
    me = lax.axis_index("seq")
    inside = [lax.rem(me, g) for g in GROUP]
    start = [me - i for i in inside]

    level1 = jnp.int32(-1)
    head1 = jnp.int32(0)
    level2 = jnp.int32(-1)
    head2 = jnp.int32(0)
    for level in range(LEVELS):
        for head in range(HEADS):
            held = inside[level] == PLACE[level][head]
            if SLOT[level][head] == 1:
                level1 = jnp.where(held, level, level1)
                head1 = jnp.where(held, head, head1)
            elif SLOT[level][head] == 2:
                level2 = jnp.where(held, level, level2)
                head2 = jnp.where(held, head, head2)

    def level_of(u):
        return jnp.where(u == 0, 0, jnp.where(u == 1, level1, level2))

    def head_of(u):
        return jnp.where(u == 0, inside[0], jnp.where(u == 1, head1, head2))

    def tiles_of(u):
        return jnp.where(u == 0, TILE_BASE[0], jnp.where(u == 1, TILE_BASE[1], TILE_BASE[2]))

    def push(src, dst, target, send_sem, recv_sem):
        @pl.when(target != me)
        def _():
            pltpu.make_async_remote_copy(
                src_ref=src, dst_ref=dst, send_sem=send_sem, recv_sem=recv_sem,
                device_id={"seq": target}, device_id_type=MESH,
            ).start()

        @pl.when(target == me)
        def _():
            pltpu.make_async_copy(src, dst, recv_sem).start()

    def sent(src, target, send_sem):
        @pl.when(target != me)
        def _():
            pltpu.make_async_copy(src, src, send_sem).wait()

    def arrived(ref, sem):
        pltpu.make_async_copy(ref, ref, sem).wait()

    barrier = pltpu.get_barrier_semaphore()

    def greet(i, carry):
        pl.semaphore_signal(
            barrier, inc=1, device_id={"seq": lax.rem(me + 1 + i, SEQ_DEVICES)}, device_id_type=MESH
        )
        return carry

    lax.fori_loop(0, SEQ_DEVICES - 1, greet, 0)

    row = lax.broadcasted_iota(jnp.int32, (TOKENS, TOKENS), 0)
    col = lax.broadcasted_iota(jnp.int32, (TOKENS, TOKENS), 1)
    upper8 = lax.broadcasted_iota(jnp.int32, (16, 256), 0) < 8

    def select(head, carry):
        lanes = pl.ds(pl.multiple_of(head * DH, DH), DH)
        pair0 = jnp.concatenate([q_ref[:, lanes], k_ref[:, lanes]], axis=1)
        pair1 = jnp.concatenate([v_ref[:, lanes], g_ref[:, lanes]], axis=1)
        pick = (position(row, off_ref, head) == col).astype(F32).astype(BF16)
        sel0 = nn(pick, pair0)
        sel1 = nn(pick, pair1)
        s0[head, 0] = pair0
        s0[head, 1] = pair1
        sbuf[head, 0] = sel0[:112].astype(BF16)
        sbuf[head, 1] = sel1[:112].astype(BF16)
        s4[head] = jnp.where(upper8, sel0[112:], sel1[112:]).astype(BF16)
        return carry

    lax.fori_loop(0, HEADS, select, 0)

    pl.semaphore_wait(barrier, SEQ_DEVICES - 1)

    def in_copy(level, head):
        slot = SLOT[level][head]
        rows = ROWS[level]
        if level == 0:
            src = s0.at[head]
        elif level < 4:
            src = sbuf.at[head, :, pl.ds(FIRST[level], rows), :]
        else:
            src = s4.at[head]
        if level < 4:
            dst = ubuf.at[slot, :, pl.ds(pl.multiple_of(inside[level] * rows, rows), rows), :]
        else:
            dst = u4.at[me]
        return src, dst, start[level] + PLACE[level][head], in_send.at[level * HEADS + head], in_recv.at[slot]

    for level in range(LEVELS):
        for head in range(HEADS):
            push(*in_copy(level, head))

    key_i = lax.broadcasted_iota(jnp.int32, (HALF, HALF), 0)
    query_i = lax.broadcasted_iota(jnp.int32, (HALF, HALF), 1)
    causal = key_i <= query_i

    def forward(u, carry):
        level = level_of(u)
        head = head_of(u)

        @pl.when((level >= 0) & (level < 4))
        def _():
            arrived(ubuf.at[u], in_recv.at[u])

        @pl.when(level == 4)
        def _():
            arrived(u4, in_recv.at[u])

            def unpack(n, c):
                block = u4[pl.ds(n * 8, 8)].astype(F32)
                rows = pl.ds(pl.multiple_of(n * 64, 64), 64)
                ubuf[u, 0, rows, :] = block[:, :8, :].reshape(64, 256).astype(BF16)
                ubuf[u, 1, rows, :] = block[:, 8:, :].reshape(64, 256).astype(BF16)
                return c

            lax.fori_loop(0, 8, unpack, 0)

        @pl.when(level >= 0)
        def _():
            for j in range(2):
                keys = HALF * (j + 1)
                cols = pl.ds(j * HALF, HALF)
                q = ubuf[u, 0, cols, :DH]
                k = ubuf[u, 0, :keys, DH:]
                v = ubuf[u, 1, :keys, :DH]
                g = ubuf[u, 1, cols, DH:]
                s = nt(k, q) * SCALE
                last = jnp.where(causal, s[j * HALF :], MASKED)
                s = last if j == 0 else jnp.concatenate([s[:HALF], last], axis=0)
                m = jnp.max(s, axis=0, keepdims=True)
                e = jnp.exp(s - m)
                den = jnp.sum(e, axis=0, keepdims=True)
                ebuf[u, :keys, cols] = e
                abuf[u, :, cols] = tn(v, e.astype(BF16))
                dp = nt(v, g)
                dbuf[u, :keys, cols] = dp
                t = jnp.sum(e * dp, axis=0, keepdims=True)
                tile = jnp.concatenate([m, den, t, jnp.zeros((5, HALF), F32)], axis=0)
                stbuf[u, 2 * j] = tile[:, :128]
                stbuf[u, 2 * j + 1] = tile[:, 128:]

            first = me - lax.rem(me, 4 << level)

            def send_stats(i, c):
                push(
                    stbuf.at[u, lax.shift_right_logical(i, level)],
                    stin.at[level * HEADS + head],
                    first + i,
                    st_send.at[tiles_of(u) + i],
                    st_recv,
                )
                return c

            lax.fori_loop(0, 4 << level, send_stats, 0)

        return carry

    lax.fori_loop(0, 3, forward, 0)

    arrived(stin, st_recv)
    lane = lax.broadcasted_iota(jnp.int32, (1, TOKENS), 1)
    spread = [None]
    stats = [stin[:HEADS]]
    for level in range(1, LEVELS):
        base = (inside[level] & ((1 << level) - 1)) * ROWS[level]
        rep = (row == base + lax.shift_right_logical(col, level)).astype(F32)
        spread.append(rep)
        tiles = stin[level * HEADS : (level + 1) * HEADS].reshape(HEADS * 8, TOKENS)
        stats.append(dot(tiles, rep, ((1,), (0,)), lax.Precision.HIGHEST).reshape(HEADS, 8, TOKENS))
    answers = [[] for _ in range(LEVELS)]
    for head in range(HEADS):
        chosen = [None] + [
            (lane & ((1 << level) - 1)) == off_ref[level, head] for level in range(1, LEVELS)
        ]
        ms = [stats[0][head, 0:1]] + [
            jnp.where(chosen[level], stats[level][head, 0:1], MASKED) for level in range(1, LEVELS)
        ]
        top = ms[0]
        for level in range(1, LEVELS):
            top = jnp.maximum(top, ms[level])
        total = jnp.zeros((1, TOKENS), F32)
        delta = jnp.zeros((1, TOKENS), F32)
        for level in range(LEVELS):
            weight = jnp.exp(ms[level] - top)
            den, t = stats[level][head, 1:2], stats[level][head, 2:3]
            if level:
                den = jnp.where(chosen[level], den, 0.0)
                t = jnp.where(chosen[level], t, 0.0)
            total = total + den * weight
            delta = delta + t * weight
        log_total = top + jnp.log(total)
        delta = delta * jnp.exp(top - log_total)
        lse_ref[head : head + 1, :] = log_total
        answer = jnp.concatenate([log_total, delta, jnp.zeros((6, TOKENS), F32)], axis=0)
        for level in range(LEVELS):
            answers[level].append(answer if level == 0 else jnp.where(chosen[level], answer, 0.0))
    for level in range(LEVELS):
        if level:
            packed = dot(
                jnp.concatenate(answers[level], axis=0), spread[level], ((1,), (1,)), lax.Precision.HIGHEST
            ).reshape(HEADS, 8, TOKENS)
        for head in range(HEADS):
            cout[level * HEADS + head] = packed[head] if level else answers[0][head]

    def c_copy(level, head):
        slot = SLOT[level][head]
        n = level * HEADS + head
        return (
            cout.at[n], cin.at[TILE_BASE[slot] + inside[level]], start[level] + PLACE[level][head],
            c_send.at[n], c_recv.at[slot],
        )

    for level in range(LEVELS):
        for head in range(HEADS):
            push(*c_copy(level, head))

    def res_copy(u, level, i, head):
        rows = ROWS[level]
        if level < 4:
            src = obuf.at[u, :, pl.ds(pl.multiple_of(i * rows, rows), rows), :]
        else:
            src = o4.at[i]
        if level == 0:
            dst, sem = r0.at[head], res_recv.at[0]
        elif level < 4:
            dst, sem = rbuf.at[head, :, pl.ds(FIRST[level], rows), :], res_recv.at[1]
        else:
            dst, sem = r4.at[head], res_recv.at[2]
        return src, dst, start[level] + i, res_send.at[tiles_of(u) + i], sem

    def backward(u, carry):
        level = level_of(u)
        head = head_of(u)
        base = tiles_of(u)
        for lv in range(LEVELS):

            @pl.when(level == lv)
            def _():
                arrived(cin.at[pl.ds(base, GROUP[lv])], c_recv.at[u])

        @pl.when(level >= 0)
        def _():
            per = lax.shift_left(1, level)
            blocks = []
            for b in range(4):
                blocks.append(
                    lax.fori_loop(
                        0, per, lambda i, c: c + cin[base + b * per + i], jnp.zeros((8, TOKENS), F32)
                    )
                )
            dk = dv = None
            for j in range(2):
                keys = HALF * (j + 1)
                cols = pl.ds(j * HALF, HALF)
                q = ubuf[u, 0, cols, :DH]
                k = ubuf[u, 0, :keys, DH:]
                g = ubuf[u, 1, cols, DH:]
                answer = jnp.concatenate(blocks[2 * j : 2 * j + 2], axis=1)
                m = jnp.concatenate([stbuf[u, 2 * j], stbuf[u, 2 * j + 1]], axis=1)[0:1]
                w = jnp.exp(m - answer[0:1])
                delta = answer[1:2]
                p = ebuf[u, :keys, cols] * w
                ds = (SCALE * p * (dbuf[u, :keys, cols] - delta)).astype(BF16)
                p = p.astype(BF16)
                o = (abuf[u, :, cols] * w).T
                dq = tn(k, ds).T
                obuf[u, 0, cols, :DH] = o.astype(BF16)
                obuf[u, 0, cols, DH:] = dq.astype(BF16)
                dkj = nn(ds, q)
                dvj = nn(p, g)
                if j == 0:
                    dk, dv = dkj, dvj
                else:
                    obuf[u, 1, :HALF, :DH] = (dk + dkj[:HALF]).astype(BF16)
                    obuf[u, 1, :HALF, DH:] = (dv + dvj[:HALF]).astype(BF16)
                    obuf[u, 1, HALF:, :DH] = dkj[HALF:].astype(BF16)
                    obuf[u, 1, HALF:, DH:] = dvj[HALF:].astype(BF16)

        @pl.when(level == 4)
        def _():
            def pack(n, c):
                rows = pl.ds(pl.multiple_of(n * 64, 64), 64)
                lo = obuf[u, 0, rows, :].astype(F32).reshape(8, 8, 256)
                hi = obuf[u, 1, rows, :].astype(F32).reshape(8, 8, 256)
                o4[pl.ds(n * 8, 8)] = jnp.concatenate([lo, hi], axis=1).astype(BF16)
                return c

            lax.fori_loop(0, 8, pack, 0)

        for lv in range(LEVELS):

            @pl.when(level == lv)
            def _():
                def send_result(i, c):
                    push(*res_copy(u, lv, i, head))
                    return c

                lax.fori_loop(0, GROUP[lv], send_result, 0)

        return carry

    lax.fori_loop(0, 3, backward, 0)

    arrived(r0, res_recv.at[0])
    arrived(rbuf, res_recv.at[1])
    arrived(r4, res_recv.at[2])

    def finish(head, carry):
        lanes = pl.ds(pl.multiple_of(head * DH, DH), DH)
        hit = position(col, off_ref, head) == row
        put0 = (hit & (col < 120)).astype(F32).astype(BF16)
        put1 = (hit & ((col < 112) | (col >= 120))).astype(F32).astype(BF16)
        four = r4[head]
        all0 = r0[head, 0].astype(F32) + nn(put0, jnp.concatenate([rbuf[head, 0], four], axis=0))
        all1 = r0[head, 1].astype(F32) + nn(put1, jnp.concatenate([rbuf[head, 1], four], axis=0))
        out_ref[:, lanes] = all0[:, :DH].astype(BF16)
        dq_ref[:, lanes] = all0[:, DH:].astype(BF16)
        dk_ref[:, lanes] = all1[:, :DH].astype(BF16)
        dv_ref[:, lanes] = all1[:, DH:].astype(BF16)
        return carry

    lax.fori_loop(0, HEADS, finish, 0)

    for level in range(LEVELS):
        for head in range(HEADS):
            src, _, target, sem, _ = in_copy(level, head)
            sent(src, target, sem)
            src, _, target, sem, _ = c_copy(level, head)
            sent(src, target, sem)

    def drain(u, carry):
        level = level_of(u)
        for lv in range(LEVELS):

            @pl.when(level == lv)
            def _():
                def one(i, c):
                    src, _, target, sem, _ = res_copy(u, lv, i, 0)
                    sent(src, target, sem)
                    sent(stbuf.at[u, 0], target, st_send.at[tiles_of(u) + i])
                    return c

                lax.fori_loop(0, GROUP[lv], one, 0)

        return carry

    lax.fori_loop(0, 3, drain, 0)


def on_device(query_in, key_in, value_in, grad_out, offsets):
    flat = jax.ShapeDtypeStruct((TOKENS, HEADS * DH), BF16)
    vmem = pl.BlockSpec(memory_space=pltpu.VMEM)
    return pl.pallas_call(
        kernel,
        out_shape=(flat, jax.ShapeDtypeStruct((HEADS, TOKENS), F32), flat, flat, flat),
        in_specs=[vmem] * 4 + [pl.BlockSpec(memory_space=pltpu.SMEM)],
        out_specs=(vmem,) * 5,
        scratch_shapes=[
            pltpu.VMEM((HEADS, 2, TOKENS, 256), BF16),
            pltpu.VMEM((HEADS, 2, 112, 256), BF16),
            pltpu.VMEM((HEADS, 16, 256), BF16),
            pltpu.VMEM((3, 2, SUB, 256), BF16),
            pltpu.VMEM((SEQ_DEVICES, 16, 256), BF16),
            pltpu.VMEM((3, SUB, SUB), F32),
            pltpu.VMEM((3, SUB, SUB), F32),
            pltpu.VMEM((3, DH, SUB), F32),
            pltpu.VMEM((3, 4, 8, 128), F32),
            pltpu.VMEM((LEVELS * HEADS, 8, 128), F32),
            pltpu.VMEM((LEVELS * HEADS, 8, 128), F32),
            pltpu.VMEM((76, 8, 128), F32),
            pltpu.VMEM((3, 2, SUB, 256), BF16),
            pltpu.VMEM((SEQ_DEVICES, 16, 256), BF16),
            pltpu.VMEM((HEADS, 2, TOKENS, 256), BF16),
            pltpu.VMEM((HEADS, 2, 112, 256), BF16),
            pltpu.VMEM((HEADS, 16, 256), BF16),
            pltpu.SemaphoreType.DMA((LEVELS * HEADS,)),
            pltpu.SemaphoreType.DMA((3,)),
            pltpu.SemaphoreType.DMA((76,)),
            pltpu.SemaphoreType.DMA,
            pltpu.SemaphoreType.DMA((LEVELS * HEADS,)),
            pltpu.SemaphoreType.DMA((3,)),
            pltpu.SemaphoreType.DMA((76,)),
            pltpu.SemaphoreType.DMA((3,)),
        ],
        compiler_params=pltpu.CompilerParams(
            collective_id=0, has_side_effects=True, vmem_limit_bytes=48 * 1024 * 1024
        ),
    )(query_in, key_in, value_in, grad_out, offsets)


def solution(mesh):
    return jax.shard_map(
        on_device,
        mesh=mesh,
        in_specs=(P("seq", "head"),) * 4 + (P(None, "head"),),
        out_specs=(P("seq", "head"), P("head", "seq")) + (P("seq", "head"),) * 3,
        check_vma=False,
    )
```

```python
import jax
import jax.numpy as jnp
from jax import lax
from jax.experimental import pallas as pl
from jax.experimental.pallas import tpu as pltpu
from jax.sharding import PartitionSpec as P

MESH = pl.DeviceIdType.MESH
F32 = jnp.float32
BF16 = jnp.bfloat16

SEQ_DEVICES = 64
HEADS = 5
LEVELS = 5
DH = 128
TOKENS = 128
SUB = 512
HALF = 256
SCALE = DH ** (-0.5)
MASKED = -1e30

GROUP = [2] + [4 << level for level in range(1, LEVELS)]
ROWS = [TOKENS >> level for level in range(LEVELS)]
PLACE = [
    None,
    [0, 2, 3, 4, 5],
    [0, 6, 7, 8, 9],
    [5, 15, 17, 28, 31],
    [1, 12, 33, 45, 52],
]
SLOTS = 5
FIRST = [0, 0, 64, 96, 112]
TILES = 2 * 3 + 8 + 64


def dot(a, b, dims, precision=None):
    return lax.dot_general(a, b, (dims, ((), ())), precision=precision, preferred_element_type=F32)


def nn(a, b):
    return dot(a, b, ((1,), (0,)))


def nt(a, b):
    return dot(a, b, ((1,), (1,)))


def tn(a, b):
    return dot(a, b, ((0,), (0,)))


def position(index, off_ref, head):
    return jnp.where(
        index < 64,
        2 * index + off_ref[1, head],
        jnp.where(
            index < 96,
            4 * (index - 64) + off_ref[2, head],
            jnp.where(
                index < 112,
                8 * (index - 96) + off_ref[3, head],
                16 * ((index - 112) & 7) + off_ref[4, head],
            ),
        ),
    )


def kernel(
    q_ref, k_ref, v_ref, g_ref, off_ref,
    out_ref, lse_ref, dq_ref, dk_ref, dv_ref,
    s0, sbuf, s4, ubuf, u4, ebuf, dbuf, abuf, stbuf, stin, cout, cin, acc, obuf, o4, r0, r0b, rbuf, r4,
    load_sem, in_send, kv_send, in_recv, kv_recv, st_send, st_recv, c_send, c_recv, res_send, res_kv_send, res_recv,
):
    me = lax.axis_index("seq")
    inside = [lax.rem(me, g) for g in GROUP]
    start = [me - i for i in inside]
    core = inside[0]
    upper = lax.rem(lax.div(me, 2), 2)

    level3 = jnp.int32(-1)
    head3 = jnp.int32(0)
    level4 = jnp.int32(-1)
    head4 = jnp.int32(0)
    for level in range(1, LEVELS):
        for head in range(HEADS):
            held = inside[level] == PLACE[level][head]
            if level == 1:
                level3 = jnp.where(held, level, level3)
                head3 = jnp.where(held, head, head3)
            else:
                level4 = jnp.where(held, level, level4)
                head4 = jnp.where(held, head, head4)

    def level_of(u):
        local = jnp.where((u == 2) & (core == 1), -1, 0)
        return jnp.where(u < 3, local, jnp.where(u == 3, level3, level4))

    def head_of(u):
        local = jnp.where(u == 2, 4, u + 2 * core)
        return jnp.where(u < 3, local, jnp.where(u == 3, head3, head4))

    def tiles_of(u):
        return jnp.where(u < 3, 2 * u, jnp.where(u == 3, 6, 14))

    def holder(level, head):
        if level == 0:
            return start[0] + (lax.div(head, 2) & 1), (head & 1) + 2 * lax.div(head, 4)
        place = jnp.int32(0)
        for h in range(HEADS):
            place = jnp.where(head == h, PLACE[level][h], place)
        return start[level] + place, 3 if level == 1 else 4

    def remote(src, dst, target, send_sem, recv_sem):
        pltpu.make_async_remote_copy(
            src_ref=src, dst_ref=dst, send_sem=send_sem, recv_sem=recv_sem,
            device_id={"seq": target}, device_id_type=MESH,
        ).start()

    def push(src, dst, target, send_sem, recv_sem):
        @pl.when(target != me)
        def _():
            remote(src, dst, target, send_sem, recv_sem)

        @pl.when(target == me)
        def _():
            pltpu.make_async_copy(src, dst, recv_sem).start()

    def done(src, send_sem):
        pltpu.make_async_copy(src, src, send_sem).wait()

    def sent(src, target, send_sem):
        @pl.when(target != me)
        def _():
            done(src, send_sem)

    arrived = done

    def load(head, carry):
        lanes = pl.ds(pl.multiple_of(head * DH, DH), DH)
        for pair, half, ref in ((0, 0, q_ref), (0, 1, g_ref), (1, 0, k_ref), (1, 1, v_ref)):
            pltpu.make_async_copy(
                ref.at[:, lanes], s0.at[head, pair, :, pl.ds(half * DH, DH)], load_sem
            ).start()
        return carry

    lax.fori_loop(0, HEADS, load, 0)

    barrier = pltpu.get_barrier_semaphore()

    def greet(i, carry):
        pl.semaphore_signal(
            barrier, inc=1, device_id={"seq": lax.rem(me + 1 + i, SEQ_DEVICES)}, device_id_type=MESH
        )
        return carry

    lax.fori_loop(0, SEQ_DEVICES - 1, greet, 0)

    row = lax.broadcasted_iota(jnp.int32, (TOKENS, TOKENS), 0)
    col = lax.broadcasted_iota(jnp.int32, (TOKENS, TOKENS), 1)
    upper8 = lax.broadcasted_iota(jnp.int32, (16, 256), 0) < 8
    arrived(s0, load_sem)

    def select(head, carry):
        pick = (position(row, off_ref, head) == col).astype(F32).astype(BF16)
        sel0 = nn(pick, s0[head, 0])
        sel1 = nn(pick, s0[head, 1])
        sbuf[head, 0] = sel0[:112].astype(BF16)
        sbuf[head, 1] = sel1[:112].astype(BF16)
        s4[head] = jnp.where(upper8, sel0[112:], sel1[112:]).astype(BF16)
        return carry

    lax.fori_loop(0, HEADS, select, 0)

    pl.semaphore_wait(barrier, SEQ_DEVICES - 1)

    def in_copy(level, head):
        rows = ROWS[level]
        target, slot = holder(level, head)
        if level == 0:
            src = s0.at[head]
            at = upper * HALF + core * TOKENS
        elif level < 4:
            src = sbuf.at[head, :, pl.ds(FIRST[level], rows), :]
            at = inside[level] * rows
        else:
            src = s4.at[head]
        if level < 4:
            dst = ubuf.at[slot, :, pl.ds(pl.multiple_of(at, rows), rows), :]
        else:
            dst = u4.at[me]
        return src, dst, target, in_send.at[level * HEADS + head], in_recv.at[slot]

    def kv_copy(head):
        target, slot = holder(0, head)
        at = pl.ds(pl.multiple_of(core * TOKENS, TOKENS), TOKENS)
        return s0.at[head, 1], ubuf.at[slot, 1, at, :], target + 2, kv_send.at[head], kv_recv.at[slot]

    turn = lax.div(me, 2)
    for level in range(LEVELS - 1, -1, -1):

        def send_rows(i, carry):
            head = lax.rem(turn + i, HEADS)
            push(*in_copy(level, head))
            if level == 0:

                @pl.when(upper == 0)
                def _():
                    remote(*kv_copy(head))

            return carry

        lax.fori_loop(0, HEADS, send_rows, 0)

    key_i = lax.broadcasted_iota(jnp.int32, (HALF, HALF), 0)
    query_i = lax.broadcasted_iota(jnp.int32, (HALF, HALF), 1)
    causal = key_i <= query_i

    def does(level, j):
        return (level > 0) | ((level == 0) & (upper == j))

    def forward(step, carry):
        u = SLOTS - 1 - step
        level = level_of(u)
        head = head_of(u)

        @pl.when(level == 0)
        def _():
            arrived(ubuf.at[u, :, pl.ds(0, HALF), :], in_recv.at[u])

            @pl.when(upper == 1)
            def _():
                arrived(ubuf.at[u, 1, pl.ds(0, HALF), :], kv_recv.at[u])

        @pl.when((level > 0) & (level < 4))
        def _():
            arrived(ubuf.at[u], in_recv.at[u])

        @pl.when(level == 4)
        def _():
            arrived(u4, in_recv.at[u])

            def unpack(n, c):
                block = u4[pl.ds(n * 8, 8)].astype(F32)
                rows = pl.ds(pl.multiple_of(n * 64, 64), 64)
                ubuf[u, 0, rows, :] = block[:, :8, :].reshape(64, 256).astype(BF16)
                ubuf[u, 1, rows, :] = block[:, 8:, :].reshape(64, 256).astype(BF16)
                return c

            lax.fori_loop(0, 8, unpack, 0)

        for j in range(2):

            @pl.when(does(level, j))
            def _():
                keys = HALF * (j + 1)
                cols = pl.ds(j * HALF, HALF)
                q = ubuf[u, 0, cols, :DH]
                g = ubuf[u, 0, cols, DH:]
                k = ubuf[u, 1, :keys, :DH]
                v = ubuf[u, 1, :keys, DH:]
                s = nt(k, q) * SCALE
                last = jnp.where(causal, s[j * HALF :], MASKED)
                s = last if j == 0 else jnp.concatenate([s[:HALF], last], axis=0)
                m = jnp.max(s, axis=0, keepdims=True)
                e = jnp.exp(s - m)
                den = jnp.sum(e, axis=0, keepdims=True)
                ebuf[u, :keys, cols] = e
                abuf[u, :, cols] = tn(v, e.astype(BF16))
                dp = nt(v, g)
                dbuf[u, :keys, cols] = dp
                t = jnp.sum(e * dp, axis=0, keepdims=True)
                tile = jnp.concatenate([m, den, t, jnp.zeros((5, HALF), F32)], axis=0)
                stbuf[u, 2 * j] = tile[:, :128]
                stbuf[u, 2 * j + 1] = tile[:, 128:]

        @pl.when(level >= 0)
        def _():
            count = jnp.where(level == 0, 2, 4 << level)
            first = me - lax.rem(me, count)
            block = jnp.where(level == 0, 2 * upper, 0)

            def send_stats(i, c):
                push(
                    stbuf.at[u, block + lax.shift_right_logical(i, level)],
                    stin.at[level * HEADS + head],
                    first + i,
                    st_send.at[tiles_of(u) + i],
                    st_recv,
                )
                return c

            lax.fori_loop(0, count, send_stats, 0)

        return carry

    lax.fori_loop(0, SLOTS, forward, 0)

    arrived(stin, st_recv)
    lane = lax.broadcasted_iota(jnp.int32, (1, TOKENS), 1)
    spread = [None]
    stats = [stin[:HEADS]]
    for level in range(1, LEVELS):
        base = (inside[level] & ((1 << level) - 1)) * ROWS[level]
        rep = (row == base + lax.shift_right_logical(col, level)).astype(F32)
        spread.append(rep)
        tiles = stin[level * HEADS : (level + 1) * HEADS].reshape(HEADS * 8, TOKENS)
        stats.append(dot(tiles, rep, ((1,), (0,)), lax.Precision.HIGHEST).reshape(HEADS, 8, TOKENS))
    answers = [[] for _ in range(LEVELS)]
    for head in range(HEADS):
        chosen = [None] + [
            (lane & ((1 << level) - 1)) == off_ref[level, head] for level in range(1, LEVELS)
        ]
        ms = [stats[0][head, 0:1]] + [
            jnp.where(chosen[level], stats[level][head, 0:1], MASKED) for level in range(1, LEVELS)
        ]
        top = ms[0]
        for level in range(1, LEVELS):
            top = jnp.maximum(top, ms[level])
        total = jnp.zeros((1, TOKENS), F32)
        delta = jnp.zeros((1, TOKENS), F32)
        for level in range(LEVELS):
            weight = jnp.exp(ms[level] - top)
            den, t = stats[level][head, 1:2], stats[level][head, 2:3]
            if level:
                den = jnp.where(chosen[level], den, 0.0)
                t = jnp.where(chosen[level], t, 0.0)
            total = total + den * weight
            delta = delta + t * weight
        log_total = top + jnp.log(total)
        delta = delta * jnp.exp(top - log_total)
        lse_ref[head : head + 1, :] = log_total
        answer = jnp.concatenate([log_total, delta, jnp.zeros((6, TOKENS), F32)], axis=0)
        for level in range(LEVELS):
            answers[level].append(answer if level == 0 else jnp.where(chosen[level], answer, 0.0))

    def c_copy(level, head):
        n = level * HEADS + head
        target, slot = holder(level, head)
        return cout.at[n], cin.at[tiles_of(slot) + inside[level]], target, c_send.at[n], c_recv.at[slot]

    for level in range(LEVELS - 1, -1, -1):
        if level:
            packed = dot(
                jnp.concatenate(answers[level], axis=0), spread[level], ((1,), (1,)), lax.Precision.HIGHEST
            ).reshape(HEADS, 8, TOKENS)
        for head in range(HEADS):
            cout[level * HEADS + head] = packed[head] if level else answers[0][head]

        def send_answer(i, carry):
            push(*c_copy(level, lax.rem(turn + i, HEADS)))
            return carry

        lax.fori_loop(0, HEADS, send_answer, 0)

    def res_copy(u, level, i, head):
        rows = ROWS[level]
        if level < 4:
            at = i * rows if level else upper * HALF + i * rows
            src = obuf.at[u, :, pl.ds(pl.multiple_of(at, rows), rows), :]
        else:
            src = o4.at[i]
        if level == 0:
            dst, sem = r0.at[head], res_recv.at[0]
        elif level < 4:
            dst, sem = rbuf.at[head, :, pl.ds(FIRST[level], rows), :], res_recv.at[1]
        else:
            dst, sem = r4.at[head], res_recv.at[2]
        return src, dst, start[level] + i, res_send.at[tiles_of(u) + i], sem

    def res_kv_copy(u, i, head):
        src = obuf.at[u, 1, pl.ds(pl.multiple_of(i * TOKENS, TOKENS), TOKENS), :]
        return src, r0b.at[head], start[0] - 2 + i, res_kv_send.at[2 * u + i], res_recv.at[3]

    def backward(step, carry):
        u = SLOTS - 1 - step
        level = level_of(u)
        head = head_of(u)
        base = tiles_of(u)
        for lv in range(LEVELS):

            @pl.when(level == lv)
            def _():
                arrived(cin.at[pl.ds(base, GROUP[lv])], c_recv.at[u])

        per = lax.shift_left(1, jnp.maximum(level, 0))
        origin = jnp.where(level == 0, base - 2 * upper, base)

        for j in range(2):

            @pl.when(does(level, j))
            def _():
                blocks = []
                for b in range(2 * j, 2 * j + 2):
                    blocks.append(
                        lax.fori_loop(
                            0, per, lambda i, c: c + cin[origin + b * per + i], jnp.zeros((8, TOKENS), F32)
                        )
                    )
                keys = HALF * (j + 1)
                cols = pl.ds(j * HALF, HALF)
                q = ubuf[u, 0, cols, :DH]
                g = ubuf[u, 0, cols, DH:]
                k = ubuf[u, 1, :keys, :DH]
                answer = jnp.concatenate(blocks, axis=1)
                m = jnp.concatenate([stbuf[u, 2 * j], stbuf[u, 2 * j + 1]], axis=1)[0:1]
                w = jnp.exp(m - answer[0:1])
                delta = answer[1:2]
                p = ebuf[u, :keys, cols] * w
                ds = (SCALE * p * (dbuf[u, :keys, cols] - delta)).astype(BF16)
                p = p.astype(BF16)
                o = (abuf[u, :, cols] * w).T
                dq = tn(k, ds).T
                obuf[u, 0, cols, :DH] = o.astype(BF16)
                obuf[u, 0, cols, DH:] = dq.astype(BF16)
                dk = nn(ds, q)
                dv = nn(p, g)
                if j == 0:
                    acc[:, :DH] = dk
                    acc[:, DH:] = dv
                    obuf[u, 1, :HALF, :DH] = dk.astype(BF16)
                    obuf[u, 1, :HALF, DH:] = dv.astype(BF16)
                else:
                    both = level > 0
                    obuf[u, 1, :HALF, :DH] = (dk[:HALF] + jnp.where(both, acc[:, :DH], 0.0)).astype(BF16)
                    obuf[u, 1, :HALF, DH:] = (dv[:HALF] + jnp.where(both, acc[:, DH:], 0.0)).astype(BF16)
                    obuf[u, 1, HALF:, :DH] = dk[HALF:].astype(BF16)
                    obuf[u, 1, HALF:, DH:] = dv[HALF:].astype(BF16)

        @pl.when(level == 4)
        def _():
            def pack(n, c):
                rows = pl.ds(pl.multiple_of(n * 64, 64), 64)
                lo = obuf[u, 0, rows, :].astype(F32).reshape(8, 8, 256)
                hi = obuf[u, 1, rows, :].astype(F32).reshape(8, 8, 256)
                o4[pl.ds(n * 8, 8)] = jnp.concatenate([lo, hi], axis=1).astype(BF16)
                return c

            lax.fori_loop(0, 8, pack, 0)

        for lv in range(LEVELS):

            @pl.when(level == lv)
            def _():
                def send_result(i, c):
                    push(*res_copy(u, lv, lax.rem(i + turn, GROUP[lv]), head))
                    if lv == 0:

                        @pl.when(upper == 1)
                        def _():
                            remote(*res_kv_copy(u, i, head))

                    return c

                lax.fori_loop(0, GROUP[lv], send_result, 0)

        return carry

    lax.fori_loop(0, SLOTS, backward, 0)

    arrived(r4, res_recv.at[2])
    arrived(rbuf, res_recv.at[1])
    arrived(r0, res_recv.at[0])

    @pl.when(upper == 0)
    def _():
        arrived(r0b, res_recv.at[3])

    def finish(head, carry):
        lanes = pl.ds(pl.multiple_of(head * DH, DH), DH)
        hit = position(col, off_ref, head) == row
        put0 = (hit & (col < 120)).astype(F32).astype(BF16)
        put1 = (hit & ((col < 112) | (col >= 120))).astype(F32).astype(BF16)
        four = r4[head]
        all0 = r0[head, 0].astype(F32) + nn(put0, jnp.concatenate([rbuf[head, 0], four], axis=0))
        all1 = r0[head, 1].astype(F32) + nn(put1, jnp.concatenate([rbuf[head, 1], four], axis=0))
        all1 = all1 + jnp.where(upper == 0, r0b[head].astype(F32), 0.0)
        out_ref[:, lanes] = all0[:, :DH].astype(BF16)
        dq_ref[:, lanes] = all0[:, DH:].astype(BF16)
        dk_ref[:, lanes] = all1[:, :DH].astype(BF16)
        dv_ref[:, lanes] = all1[:, DH:].astype(BF16)
        return carry

    lax.fori_loop(0, HEADS, finish, 0)

    def drain_own(head, carry):
        for level in range(LEVELS):
            src, _, target, sem, _ = in_copy(level, head)
            sent(src, target, sem)
            src, _, target, sem, _ = c_copy(level, head)
            sent(src, target, sem)

        @pl.when(upper == 0)
        def _():
            src, _, _, sem, _ = kv_copy(head)
            done(src, sem)

        return carry

    lax.fori_loop(0, HEADS, drain_own, 0)

    def drain(u, carry):
        level = level_of(u)
        for lv in range(LEVELS):

            @pl.when(level == lv)
            def _():
                def one(i, c):
                    src, _, target, sem, _ = res_copy(u, lv, i, 0)
                    sent(src, target, sem)
                    sent(stbuf.at[u, 0], target, st_send.at[tiles_of(u) + i])
                    if lv == 0:

                        @pl.when(upper == 1)
                        def _():
                            src, _, _, sem, _ = res_kv_copy(u, i, 0)
                            done(src, sem)

                    return c

                lax.fori_loop(0, GROUP[lv], one, 0)

        return carry

    lax.fori_loop(0, SLOTS, drain, 0)


def on_device(query_in, key_in, value_in, grad_out, offsets):
    flat = jax.ShapeDtypeStruct((TOKENS, HEADS * DH), BF16)
    vmem = pl.BlockSpec(memory_space=pltpu.VMEM)
    return pl.pallas_call(
        kernel,
        out_shape=(flat, jax.ShapeDtypeStruct((HEADS, TOKENS), F32), flat, flat, flat),
        in_specs=[pl.BlockSpec(memory_space=pl.ANY)] * 4 + [pl.BlockSpec(memory_space=pltpu.SMEM)],
        out_specs=(vmem,) * 5,
        scratch_shapes=[
            pltpu.VMEM((HEADS, 2, TOKENS, 256), BF16),
            pltpu.VMEM((HEADS, 2, 112, 256), BF16),
            pltpu.VMEM((HEADS, 16, 256), BF16),
            pltpu.VMEM((SLOTS, 2, SUB, 256), BF16),
            pltpu.VMEM((SEQ_DEVICES, 16, 256), BF16),
            pltpu.VMEM((SLOTS, SUB, SUB), F32),
            pltpu.VMEM((SLOTS, SUB, SUB), F32),
            pltpu.VMEM((SLOTS, DH, SUB), F32),
            pltpu.VMEM((SLOTS, 4, 8, 128), F32),
            pltpu.VMEM((LEVELS * HEADS, 8, 128), F32),
            pltpu.VMEM((LEVELS * HEADS, 8, 128), F32),
            pltpu.VMEM((TILES, 8, 128), F32),
            pltpu.VMEM((HALF, 256), F32),
            pltpu.VMEM((SLOTS, 2, SUB, 256), BF16),
            pltpu.VMEM((SEQ_DEVICES, 16, 256), BF16),
            pltpu.VMEM((HEADS, 2, TOKENS, 256), BF16),
            pltpu.VMEM((HEADS, TOKENS, 256), BF16),
            pltpu.VMEM((HEADS, 2, 112, 256), BF16),
            pltpu.VMEM((HEADS, 16, 256), BF16),
            pltpu.SemaphoreType.DMA,
            pltpu.SemaphoreType.DMA((LEVELS * HEADS,)),
            pltpu.SemaphoreType.DMA((HEADS,)),
            pltpu.SemaphoreType.DMA((SLOTS,)),
            pltpu.SemaphoreType.DMA((3,)),
            pltpu.SemaphoreType.DMA((TILES,)),
            pltpu.SemaphoreType.DMA,
            pltpu.SemaphoreType.DMA((LEVELS * HEADS,)),
            pltpu.SemaphoreType.DMA((SLOTS,)),
            pltpu.SemaphoreType.DMA((TILES,)),
            pltpu.SemaphoreType.DMA((6,)),
            pltpu.SemaphoreType.DMA((4,)),
        ],
        compiler_params=pltpu.CompilerParams(
            collective_id=0, has_side_effects=True, vmem_limit_bytes=60 * 1024 * 1024
        ),
    )(query_in, key_in, value_in, grad_out, offsets)


def solution(mesh):
    return jax.shard_map(
        on_device,
        mesh=mesh,
        in_specs=(P("seq", "head"),) * 4 + (P(None, "head"),),
        out_specs=(P("seq", "head"), P("head", "seq")) + (P("seq", "head"),) * 3,
        check_vma=False,
    )
```

```python
import jax
import jax.numpy as jnp
from jax import lax
from jax.experimental import pallas as pl
from jax.experimental.pallas import tpu as pltpu
from jax.sharding import PartitionSpec as P

MESH = pl.DeviceIdType.MESH
F32 = jnp.float32
BF16 = jnp.bfloat16

SEQ_DEVICES = 64
HEADS = 5
LEVELS = 5
DH = 128
TOKENS = 128
SUB = 512
HALF = 256
SCALE = DH ** (-0.5)
MASKED = -1e30

GROUP = [2] + [4 << level for level in range(1, LEVELS)]
ROWS = [TOKENS >> level for level in range(LEVELS)]
PLACE = [
    None,
    [0, 2, 3, 4, 5],
    [0, 6, 7, 8, 9],
    [5, 15, 17, 28, 31],
    [1, 12, 33, 45, 52],
]
SLOTS = 5
FIRST = [0, 0, 64, 96, 112]
TILES = 2 * 3 + 8 + 64


def dot(a, b, dims):
    return lax.dot_general(a, b, (dims, ((), ())), preferred_element_type=F32)


def nn(a, b):
    return dot(a, b, ((1,), (0,)))


def nt(a, b):
    return dot(a, b, ((1,), (1,)))


def tn(a, b):
    return dot(a, b, ((0,), (0,)))


def move(tiles, rep, dims):
    rows = tiles.shape[0]
    high = tiles.astype(BF16).astype(F32)
    mid = (tiles - high).astype(BF16).astype(F32)
    low = tiles - high - mid
    out = dot(jnp.concatenate([high, mid, low], axis=0).astype(BF16), rep, dims)
    return (out[2 * rows :] + out[rows : 2 * rows]) + out[:rows]


def position(index, off_ref, head):
    return jnp.where(
        index < 64,
        2 * index + off_ref[1, head],
        jnp.where(
            index < 96,
            4 * (index - 64) + off_ref[2, head],
            jnp.where(
                index < 112,
                8 * (index - 96) + off_ref[3, head],
                16 * ((index - 112) & 7) + off_ref[4, head],
            ),
        ),
    )


def kernel(
    q_ref, k_ref, v_ref, g_ref, off_ref,
    lse_ref, r0, r0b, rbuf, r4,
    s0, sbuf, s4, ubuf, u4, ebuf, dbuf, abuf, stbuf, stin, cout, cin, acc, obuf, o4,
    load_sem, in_send, kv_send, in_recv, kv_recv, st_send, st_recv, c_send, c_recv, res_send, res_kv_send, res_recv,
):
    me = lax.axis_index("seq")
    inside = [lax.rem(me, g) for g in GROUP]
    start = [me - i for i in inside]
    core = inside[0]
    upper = lax.rem(lax.div(me, 2), 2)

    level3 = jnp.int32(-1)
    head3 = jnp.int32(0)
    level4 = jnp.int32(-1)
    head4 = jnp.int32(0)
    for level in range(1, LEVELS):
        for head in range(HEADS):
            held = inside[level] == PLACE[level][head]
            if level == 1:
                level3 = jnp.where(held, level, level3)
                head3 = jnp.where(held, head, head3)
            else:
                level4 = jnp.where(held, level, level4)
                head4 = jnp.where(held, head, head4)

    def level_of(u):
        local = jnp.where((u == 2) & (core == 1), -1, 0)
        return jnp.where(u < 3, local, jnp.where(u == 3, level3, level4))

    def head_of(u):
        local = jnp.where(u == 2, 4, u + 2 * core)
        return jnp.where(u < 3, local, jnp.where(u == 3, head3, head4))

    def tiles_of(u):
        return jnp.where(u < 3, 2 * u, jnp.where(u == 3, 6, 14))

    def holder(level, head):
        if level == 0:
            return start[0] + (lax.div(head, 2) & 1), (head & 1) + 2 * lax.div(head, 4)
        place = jnp.int32(0)
        for h in range(HEADS):
            place = jnp.where(head == h, PLACE[level][h], place)
        return start[level] + place, 3 if level == 1 else 4

    def remote(src, dst, target, send_sem, recv_sem):
        pltpu.make_async_remote_copy(
            src_ref=src, dst_ref=dst, send_sem=send_sem, recv_sem=recv_sem,
            device_id={"seq": target}, device_id_type=MESH,
        ).start()

    def push(src, dst, target, send_sem, recv_sem):
        @pl.when(target != me)
        def _():
            remote(src, dst, target, send_sem, recv_sem)

        @pl.when(target == me)
        def _():
            pltpu.make_async_copy(src, dst, recv_sem).start()

    def done(src, send_sem):
        pltpu.make_async_copy(src, src, send_sem).wait()

    def sent(src, target, send_sem):
        @pl.when(target != me)
        def _():
            done(src, send_sem)

    arrived = done

    barrier = pltpu.get_barrier_semaphore()

    def greet(i, carry):
        pl.semaphore_signal(
            barrier, inc=1, device_id={"seq": lax.rem(me + 1 + lax.rem(i + 15, 63), SEQ_DEVICES)}, device_id_type=MESH
        )
        return carry

    lax.fori_loop(0, SEQ_DEVICES - 1, greet, 0)

    def load(head, carry):
        lanes = pl.ds(pl.multiple_of(head * DH, DH), DH)
        for pair, half, ref in ((0, 0, q_ref), (0, 1, g_ref), (1, 0, k_ref), (1, 1, v_ref)):
            pltpu.make_async_copy(
                ref.at[:, lanes], s0.at[head, pair, :, pl.ds(half * DH, DH)], load_sem
            ).start()
        return carry

    lax.fori_loop(0, HEADS, load, 0)

    row = lax.broadcasted_iota(jnp.int32, (TOKENS, TOKENS), 0)
    col = lax.broadcasted_iota(jnp.int32, (TOKENS, TOKENS), 1)
    upper8 = lax.broadcasted_iota(jnp.int32, (16, 256), 0) < 8
    arrived(s0, load_sem)

    def select(head, carry):
        pick = (position(row, off_ref, head) == col).astype(F32).astype(BF16)
        sel0 = nn(pick, s0[head, 0])
        sel1 = nn(pick, s0[head, 1])
        sbuf[head, 0] = sel0[:112].astype(BF16)
        sbuf[head, 1] = sel1[:112].astype(BF16)
        s4[head] = jnp.where(upper8, sel0[112:], sel1[112:]).astype(BF16)
        return carry

    lax.fori_loop(0, HEADS, select, 0)

    pl.semaphore_wait(barrier, SEQ_DEVICES - 1)

    def in_copy(level, head):
        rows = ROWS[level]
        target, slot = holder(level, head)
        if level == 0:
            src = s0.at[head]
            at = upper * HALF + core * TOKENS
        elif level < 4:
            src = sbuf.at[head, :, pl.ds(FIRST[level], rows), :]
            at = inside[level] * rows
        else:
            src = s4.at[head]
        if level < 4:
            dst = ubuf.at[slot, :, pl.ds(pl.multiple_of(at, rows), rows), :]
        else:
            dst = u4.at[me]
        return src, dst, target, in_send.at[level * HEADS + head], in_recv.at[slot]

    def kv_copy(head):
        target, slot = holder(0, head)
        at = pl.ds(pl.multiple_of(core * TOKENS, TOKENS), TOKENS)
        return s0.at[head, 1], ubuf.at[slot, 1, at, :], target + 2, kv_send.at[head], kv_recv.at[slot]

    turn = lax.div(me, 2)
    for level in range(LEVELS - 1, -1, -1):

        def send_rows(i, carry):
            head = lax.rem(turn + i, HEADS)
            push(*in_copy(level, head))
            if level == 0:

                @pl.when(upper == 0)
                def _():
                    remote(*kv_copy(head))

            return carry

        lax.fori_loop(0, HEADS, send_rows, 0)

    key_i = lax.broadcasted_iota(jnp.int32, (HALF, HALF), 0)
    query_i = lax.broadcasted_iota(jnp.int32, (HALF, HALF), 1)
    causal = key_i <= query_i

    def does(level, j):
        return (level > 0) | ((level == 0) & (upper == j))

    def forward(step, carry):
        u = SLOTS - 1 - step
        level = level_of(u)
        head = head_of(u)

        @pl.when(level == 0)
        def _():
            arrived(ubuf.at[u, :, pl.ds(0, HALF), :], in_recv.at[u])

            @pl.when(upper == 1)
            def _():
                arrived(ubuf.at[u, 1, pl.ds(0, HALF), :], kv_recv.at[u])

        @pl.when((level > 0) & (level < 4))
        def _():
            arrived(ubuf.at[u], in_recv.at[u])

        @pl.when(level == 4)
        def _():
            arrived(u4, in_recv.at[u])

            def unpack(n, c):
                block = u4[pl.ds(n * 8, 8)].astype(F32)
                rows = pl.ds(pl.multiple_of(n * 64, 64), 64)
                ubuf[u, 0, rows, :] = block[:, :8, :].reshape(64, 256).astype(BF16)
                ubuf[u, 1, rows, :] = block[:, 8:, :].reshape(64, 256).astype(BF16)
                return c

            lax.fori_loop(0, 8, unpack, 0)

        for j in range(2):

            @pl.when(does(level, j))
            def _():
                keys = HALF * (j + 1)
                cols = pl.ds(j * HALF, HALF)
                q = ubuf[u, 0, cols, :DH]
                g = ubuf[u, 0, cols, DH:]
                k = ubuf[u, 1, :keys, :DH]
                v = ubuf[u, 1, :keys, DH:]
                s = nt(k, q) * SCALE
                last = jnp.where(causal, s[j * HALF :], MASKED)
                s = last if j == 0 else jnp.concatenate([s[:HALF], last], axis=0)
                m = jnp.max(s, axis=0, keepdims=True)
                e = jnp.exp(s - m)
                den = jnp.sum(e, axis=0, keepdims=True)
                ebuf[u, :keys, cols] = e
                abuf[u, :, cols] = tn(v, e.astype(BF16))
                dp = nt(v, g)
                dbuf[u, :keys, cols] = dp
                t = jnp.sum(e * dp, axis=0, keepdims=True)
                tile = jnp.concatenate([m, den, t, jnp.zeros((5, HALF), F32)], axis=0)
                stbuf[u, 2 * j] = tile[:, :128]
                stbuf[u, 2 * j + 1] = tile[:, 128:]

        @pl.when(level >= 0)
        def _():
            count = jnp.where(level == 0, 2, 4 << level)
            first = me - lax.rem(me, count)
            block = jnp.where(level == 0, 2 * upper, 0)

            def send_stats(i, c):
                push(
                    stbuf.at[u, block + lax.shift_right_logical(i, level)],
                    stin.at[level * HEADS + head],
                    first + i,
                    st_send.at[tiles_of(u) + i],
                    st_recv,
                )
                return c

            lax.fori_loop(0, count, send_stats, 0)

        return carry

    lax.fori_loop(0, SLOTS, forward, 0)

    arrived(stin, st_recv)
    lane = lax.broadcasted_iota(jnp.int32, (1, TOKENS), 1)
    spread = [None]
    stats = [stin[:HEADS]]
    for level in range(1, LEVELS):
        base = (inside[level] & ((1 << level) - 1)) * ROWS[level]
        rep = (row == base + lax.shift_right_logical(col, level)).astype(F32).astype(BF16)
        spread.append(rep)
        tiles = stin[level * HEADS : (level + 1) * HEADS].reshape(HEADS * 8, TOKENS)
        stats.append(move(tiles, rep, ((1,), (0,))).reshape(HEADS, 8, TOKENS))
    answers = [[] for _ in range(LEVELS)]
    for head in range(HEADS):
        chosen = [None] + [
            (lane & ((1 << level) - 1)) == off_ref[level, head] for level in range(1, LEVELS)
        ]
        ms = [stats[0][head, 0:1]] + [
            jnp.where(chosen[level], stats[level][head, 0:1], MASKED) for level in range(1, LEVELS)
        ]
        top = ms[0]
        for level in range(1, LEVELS):
            top = jnp.maximum(top, ms[level])
        total = jnp.zeros((1, TOKENS), F32)
        delta = jnp.zeros((1, TOKENS), F32)
        for level in range(LEVELS):
            weight = jnp.exp(ms[level] - top)
            den, t = stats[level][head, 1:2], stats[level][head, 2:3]
            if level:
                den = jnp.where(chosen[level], den, 0.0)
                t = jnp.where(chosen[level], t, 0.0)
            total = total + den * weight
            delta = delta + t * weight
        log_total = top + jnp.log(total)
        delta = delta * jnp.exp(top - log_total)
        lse_ref[head : head + 1, :] = log_total
        answer = jnp.concatenate([log_total, delta, jnp.zeros((6, TOKENS), F32)], axis=0)
        for level in range(LEVELS):
            answers[level].append(answer if level == 0 else jnp.where(chosen[level], answer, 0.0))

    def c_copy(level, head):
        n = level * HEADS + head
        target, slot = holder(level, head)
        return cout.at[n], cin.at[tiles_of(slot) + inside[level]], target, c_send.at[n], c_recv.at[slot]

    for level in range(LEVELS - 1, -1, -1):
        if level:
            packed = move(jnp.concatenate(answers[level], axis=0), spread[level], ((1,), (1,)))
            packed = packed.reshape(HEADS, 8, TOKENS)
        for head in range(HEADS):
            cout[level * HEADS + head] = packed[head] if level else answers[0][head]

        def send_answer(i, carry):
            push(*c_copy(level, lax.rem(turn + i, HEADS)))
            return carry

        lax.fori_loop(0, HEADS, send_answer, 0)

    def res_copy(u, level, i, head):
        rows = ROWS[level]
        if level < 4:
            at = i * rows if level else upper * HALF + i * rows
            src = obuf.at[u, :, pl.ds(pl.multiple_of(at, rows), rows), :]
        else:
            src = o4.at[i]
        if level == 0:
            dst, sem = r0.at[head], res_recv.at[0]
        elif level < 4:
            dst, sem = rbuf.at[head, :, pl.ds(FIRST[level], rows), :], res_recv.at[1]
        else:
            dst, sem = r4.at[head], res_recv.at[2]
        return src, dst, start[level] + i, res_send.at[tiles_of(u) + i], sem

    def res_kv_copy(u, i, head):
        src = obuf.at[u, 1, pl.ds(pl.multiple_of(i * TOKENS, TOKENS), TOKENS), :]
        return src, r0b.at[head], start[0] - 2 + i, res_kv_send.at[2 * u + i], res_recv.at[3]

    def backward(u, carry):
        level = level_of(u)
        head = head_of(u)
        base = tiles_of(u)
        for lv in range(LEVELS):

            @pl.when(level == lv)
            def _():
                arrived(cin.at[pl.ds(base, GROUP[lv])], c_recv.at[u])

        per = lax.shift_left(1, jnp.maximum(level, 0))
        origin = jnp.where(level == 0, base - 2 * upper, base)

        for j in range(2):

            @pl.when(does(level, j))
            def _():
                blocks = []
                for b in range(2 * j, 2 * j + 2):
                    blocks.append(
                        lax.fori_loop(
                            0, per, lambda i, c: c + cin[origin + b * per + i], jnp.zeros((8, TOKENS), F32)
                        )
                    )
                keys = HALF * (j + 1)
                cols = pl.ds(j * HALF, HALF)
                q = ubuf[u, 0, cols, :DH]
                g = ubuf[u, 0, cols, DH:]
                k = ubuf[u, 1, :keys, :DH]
                answer = jnp.concatenate(blocks, axis=1)
                m = jnp.concatenate([stbuf[u, 2 * j], stbuf[u, 2 * j + 1]], axis=1)[0:1]
                w = jnp.exp(m - answer[0:1])
                delta = answer[1:2]
                p = ebuf[u, :keys, cols] * w
                ds = (SCALE * p * (dbuf[u, :keys, cols] - delta)).astype(BF16)
                p = p.astype(BF16)
                o = (abuf[u, :, cols] * w).T
                dq = tn(k, ds).T
                obuf[u, 0, cols, :DH] = o.astype(BF16)
                obuf[u, 0, cols, DH:] = dq.astype(BF16)
                dk = nn(ds, q)
                dv = nn(p, g)
                if j == 0:
                    acc[:, :DH] = dk
                    acc[:, DH:] = dv
                    obuf[u, 1, :HALF, :DH] = dk.astype(BF16)
                    obuf[u, 1, :HALF, DH:] = dv.astype(BF16)
                else:
                    both = level > 0
                    obuf[u, 1, :HALF, :DH] = (dk[:HALF] + jnp.where(both, acc[:, :DH], 0.0)).astype(BF16)
                    obuf[u, 1, :HALF, DH:] = (dv[:HALF] + jnp.where(both, acc[:, DH:], 0.0)).astype(BF16)
                    obuf[u, 1, HALF:, :DH] = dk[HALF:].astype(BF16)
                    obuf[u, 1, HALF:, DH:] = dv[HALF:].astype(BF16)

        @pl.when(level == 4)
        def _():
            def pack(n, c):
                rows = pl.ds(pl.multiple_of(n * 64, 64), 64)
                lo = obuf[u, 0, rows, :].astype(F32).reshape(8, 8, 256)
                hi = obuf[u, 1, rows, :].astype(F32).reshape(8, 8, 256)
                o4[pl.ds(n * 8, 8)] = jnp.concatenate([lo, hi], axis=1).astype(BF16)
                return c

            lax.fori_loop(0, 8, pack, 0)

        for lv in range(LEVELS):

            @pl.when(level == lv)
            def _():
                def send_result(i, c):
                    push(*res_copy(u, lv, lax.rem(i + turn, GROUP[lv]), head))
                    if lv == 0:

                        @pl.when(upper == 1)
                        def _():
                            remote(*res_kv_copy(u, i, head))

                    return c

                lax.fori_loop(0, GROUP[lv], send_result, 0)

        return carry

    lax.fori_loop(0, SLOTS, backward, 0)

    arrived(r4, res_recv.at[2])
    arrived(rbuf, res_recv.at[1])
    arrived(r0, res_recv.at[0])

    @pl.when(upper == 0)
    def _():
        arrived(r0b, res_recv.at[3])

    def drain_own(head, carry):
        for level in range(LEVELS):
            src, _, target, sem, _ = in_copy(level, head)
            sent(src, target, sem)
            src, _, target, sem, _ = c_copy(level, head)
            sent(src, target, sem)

        @pl.when(upper == 0)
        def _():
            src, _, _, sem, _ = kv_copy(head)
            done(src, sem)

        return carry

    lax.fori_loop(0, HEADS, drain_own, 0)

    def drain(u, carry):
        level = level_of(u)
        for lv in range(LEVELS):

            @pl.when(level == lv)
            def _():
                def one(i, c):
                    src, _, target, sem, _ = res_copy(u, lv, i, 0)
                    sent(src, target, sem)
                    sent(stbuf.at[u, 0], target, st_send.at[tiles_of(u) + i])
                    if lv == 0:

                        @pl.when(upper == 1)
                        def _():
                            src, _, _, sem, _ = res_kv_copy(u, i, 0)
                            done(src, sem)

                    return c

                lax.fori_loop(0, GROUP[lv], one, 0)

        return carry

    lax.fori_loop(0, SLOTS, drain, 0)


def finish(off_ref, lse_ref, r0, r0b, rbuf, r4, out_ref, log_ref, dq_ref, dk_ref, dv_ref):
    head = pl.program_id(0)
    upper = lax.rem(lax.div(lax.axis_index("seq"), 2), 2)
    row = lax.broadcasted_iota(jnp.int32, (TOKENS, TOKENS), 0)
    col = lax.broadcasted_iota(jnp.int32, (TOKENS, TOKENS), 1)
    hit = position(col, off_ref, head) == row
    put0 = (hit & (col < 120)).astype(F32).astype(BF16)
    put1 = (hit & ((col < 112) | (col >= 120))).astype(F32).astype(BF16)
    four = r4[0]
    all0 = r0[0, 0].astype(F32) + nn(put0, jnp.concatenate([rbuf[0, 0], four], axis=0))
    all1 = r0[0, 1].astype(F32) + nn(put1, jnp.concatenate([rbuf[0, 1], four], axis=0))
    all1 = all1 + jnp.where(upper == 0, r0b[0].astype(F32), 0.0)
    out_ref[...] = all0[:, :DH].astype(BF16)
    dq_ref[...] = all0[:, DH:].astype(BF16)
    dk_ref[...] = all1[:, :DH].astype(BF16)
    dv_ref[...] = all1[:, DH:].astype(BF16)
    log_ref[...] = lse_ref[...]


def on_device(query_in, key_in, value_in, grad_out, offsets):
    hbm = pl.BlockSpec(memory_space=pl.ANY)
    smem = pl.BlockSpec(memory_space=pltpu.SMEM)
    parts = pl.pallas_call(
        kernel,
        out_shape=(
            jax.ShapeDtypeStruct((HEADS, TOKENS), F32),
            jax.ShapeDtypeStruct((HEADS, 2, TOKENS, 256), BF16),
            jax.ShapeDtypeStruct((HEADS, TOKENS, 256), BF16),
            jax.ShapeDtypeStruct((HEADS, 2, 112, 256), BF16),
            jax.ShapeDtypeStruct((HEADS, 16, 256), BF16),
        ),
        in_specs=[hbm] * 4 + [smem],
        out_specs=(pl.BlockSpec(memory_space=pltpu.VMEM),) + (hbm,) * 4,
        scratch_shapes=[
            pltpu.VMEM((HEADS, 2, TOKENS, 256), BF16),
            pltpu.VMEM((HEADS, 2, 112, 256), BF16),
            pltpu.VMEM((HEADS, 16, 256), BF16),
            pltpu.VMEM((SLOTS, 2, SUB, 256), BF16),
            pltpu.VMEM((SEQ_DEVICES, 16, 256), BF16),
            pltpu.VMEM((SLOTS, SUB, SUB), F32),
            pltpu.VMEM((SLOTS, SUB, SUB), F32),
            pltpu.VMEM((SLOTS, DH, SUB), F32),
            pltpu.VMEM((SLOTS, 4, 8, 128), F32),
            pltpu.VMEM((LEVELS * HEADS, 8, 128), F32),
            pltpu.VMEM((LEVELS * HEADS, 8, 128), F32),
            pltpu.VMEM((TILES, 8, 128), F32),
            pltpu.VMEM((HALF, 256), F32),
            pltpu.VMEM((SLOTS, 2, SUB, 256), BF16),
            pltpu.VMEM((SEQ_DEVICES, 16, 256), BF16),
            pltpu.SemaphoreType.DMA,
            pltpu.SemaphoreType.DMA((LEVELS * HEADS,)),
            pltpu.SemaphoreType.DMA((HEADS,)),
            pltpu.SemaphoreType.DMA((SLOTS,)),
            pltpu.SemaphoreType.DMA((3,)),
            pltpu.SemaphoreType.DMA((TILES,)),
            pltpu.SemaphoreType.DMA,
            pltpu.SemaphoreType.DMA((LEVELS * HEADS,)),
            pltpu.SemaphoreType.DMA((SLOTS,)),
            pltpu.SemaphoreType.DMA((TILES,)),
            pltpu.SemaphoreType.DMA((6,)),
            pltpu.SemaphoreType.DMA((4,)),
        ],
        compiler_params=pltpu.CompilerParams(
            collective_id=0, has_side_effects=True, vmem_limit_bytes=60 * 1024 * 1024
        ),
    )(query_in, key_in, value_in, grad_out, offsets)
    flat = jax.ShapeDtypeStruct((TOKENS, HEADS * DH), BF16)
    lanes = pl.BlockSpec((TOKENS, DH), lambda h: (0, h))
    return pl.pallas_call(
        finish,
        grid=(HEADS,),
        out_shape=(flat, jax.ShapeDtypeStruct((HEADS, TOKENS), F32), flat, flat, flat),
        in_specs=[
            smem,
            pl.BlockSpec((HEADS, TOKENS), lambda h: (0, 0)),
            pl.BlockSpec((1, 2, TOKENS, 256), lambda h: (h, 0, 0, 0)),
            pl.BlockSpec((1, TOKENS, 256), lambda h: (h, 0, 0)),
            pl.BlockSpec((1, 2, 112, 256), lambda h: (h, 0, 0, 0)),
            pl.BlockSpec((1, 16, 256), lambda h: (h, 0, 0)),
        ],
        out_specs=(lanes, pl.BlockSpec((HEADS, TOKENS), lambda h: (0, 0)), lanes, lanes, lanes),
    )(offsets, *parts)


def solution(mesh):
    return jax.shard_map(
        on_device,
        mesh=mesh,
        in_specs=(P("seq", "head"),) * 4 + (P(None, "head"),),
        out_specs=(P("seq", "head"), P("head", "seq")) + (P("seq", "head"),) * 3,
        check_vma=False,
    )
```

```python
import jax
import jax.numpy as jnp
from jax import lax
from jax.experimental import pallas as pl
from jax.experimental.pallas import tpu as pltpu
from jax.sharding import PartitionSpec as P

MESH = pl.DeviceIdType.MESH
F32 = jnp.float32
BF16 = jnp.bfloat16

SEQ_DEVICES = 64
HEADS = 5
LEVELS = 5
DH = 128
TOKENS = 128
SUB = 512
HALF = 256
SCALE = DH ** (-0.5)
MASKED = -1e30

GROUP = [2] + [4 << level for level in range(1, LEVELS)]
ROWS = [TOKENS >> level for level in range(LEVELS)]
PLACE = [
    None,
    [0, 2, 3, 4, 5],
    [0, 6, 7, 8, 9],
    [5, 15, 17, 28, 31],
    [1, 12, 33, 45, 52],
]
SLOTS = 5
FIRST = [0, 0, 64, 96, 112]
TILES = 2 * 3 + 8 + 64


def dot(a, b, dims):
    return lax.dot_general(a, b, (dims, ((), ())), preferred_element_type=F32)


def nn(a, b):
    return dot(a, b, ((1,), (0,)))


def nt(a, b):
    return dot(a, b, ((1,), (1,)))


def tn(a, b):
    return dot(a, b, ((0,), (0,)))


def move(tiles, rep, dims):
    rows = tiles.shape[0]
    high = tiles.astype(BF16).astype(F32)
    mid = (tiles - high).astype(BF16).astype(F32)
    low = tiles - high - mid
    out = dot(jnp.concatenate([high, mid, low], axis=0).astype(BF16), rep, dims)
    return (out[2 * rows :] + out[rows : 2 * rows]) + out[:rows]


def position(index, off_ref, head):
    return jnp.where(
        index < 64,
        2 * index + off_ref[1, head],
        jnp.where(
            index < 96,
            4 * (index - 64) + off_ref[2, head],
            jnp.where(
                index < 112,
                8 * (index - 96) + off_ref[3, head],
                16 * ((index - 112) & 7) + off_ref[4, head],
            ),
        ),
    )


def kernel(
    q_ref, k_ref, v_ref, g_ref, off_ref,
    lse_ref, r0, r0b, rbuf, r4,
    s0, sbuf, s4, ubuf, u4, ebuf, dbuf, abuf, stbuf, stin, cout, cin, acc, obuf, o4,
    load_sem, in_send, kv_send, in_recv, kv_recv, st_send, st_recv, c_send, c_recv, res_send, res_kv_send, res_recv,
):
    me = lax.axis_index("seq")
    inside = [lax.rem(me, g) for g in GROUP]
    start = [me - i for i in inside]
    core = inside[0]
    upper = lax.rem(lax.div(me, 2), 2)

    level3 = jnp.int32(-1)
    head3 = jnp.int32(0)
    level4 = jnp.int32(-1)
    head4 = jnp.int32(0)
    for level in range(1, LEVELS):
        for head in range(HEADS):
            held = inside[level] == PLACE[level][head]
            if level == 1:
                level3 = jnp.where(held, level, level3)
                head3 = jnp.where(held, head, head3)
            else:
                level4 = jnp.where(held, level, level4)
                head4 = jnp.where(held, head, head4)

    def level_of(u):
        local = jnp.where((u == 2) & (core == 1), -1, 0)
        return jnp.where(u < 3, local, jnp.where(u == 3, level3, level4))

    def head_of(u):
        local = jnp.where(u == 2, 4, u + 2 * core)
        return jnp.where(u < 3, local, jnp.where(u == 3, head3, head4))

    def tiles_of(u):
        return jnp.where(u < 3, 2 * u, jnp.where(u == 3, 6, 14))

    def holder(level, head):
        if level == 0:
            return start[0] + (lax.div(head, 2) & 1), (head & 1) + 2 * lax.div(head, 4)
        place = jnp.int32(0)
        for h in range(HEADS):
            place = jnp.where(head == h, PLACE[level][h], place)
        return start[level] + place, 3 if level == 1 else 4

    def remote(src, dst, target, send_sem, recv_sem):
        pltpu.make_async_remote_copy(
            src_ref=src, dst_ref=dst, send_sem=send_sem, recv_sem=recv_sem,
            device_id={"seq": target}, device_id_type=MESH,
        ).start()

    def push(src, dst, target, send_sem, recv_sem):
        @pl.when(target != me)
        def _():
            remote(src, dst, target, send_sem, recv_sem)

        @pl.when(target == me)
        def _():
            pltpu.make_async_copy(src, dst, recv_sem).start()

    def done(src, send_sem):
        pltpu.make_async_copy(src, src, send_sem).wait()

    def sent(src, target, send_sem):
        @pl.when(target != me)
        def _():
            done(src, send_sem)

    arrived = done

    barrier = pltpu.get_barrier_semaphore()

    def greet(target):
        pl.semaphore_signal(barrier, inc=1, device_id={"seq": target}, device_id_type=MESH)

    def greet_members(count):
        first = me - lax.rem(me, count)

        def one(i, carry):
            greet(first + lax.rem(me - first + i, count))
            return carry

        lax.fori_loop(1, count, one, 0)

    other = me - 2 * upper - core + 2 - 2 * upper
    greet(start[0] + 1 - core)
    greet(other)
    greet(other + 1)
    greetings = jnp.int32(3)
    for level in range(LEVELS - 1, 0, -1):

        def greet_holder(head, count):
            target, _ = holder(level, head)

            @pl.when(target != me)
            def _():
                greet(target)

            return count + jnp.where(target != me, 1, 0)

        greetings = lax.fori_loop(0, HEADS, greet_holder, greetings)
    for level in (level4, level3):

        @pl.when(level > 0)
        def _():
            greet_members(4 << level)

        greetings = greetings + jnp.where(level > 0, lax.shift_left(4, jnp.maximum(level, 0)) - 1, 0)

    def load(head, carry):
        lanes = pl.ds(pl.multiple_of(head * DH, DH), DH)
        for pair, half, ref in ((0, 0, q_ref), (0, 1, g_ref), (1, 0, k_ref), (1, 1, v_ref)):
            pltpu.make_async_copy(
                ref.at[:, lanes], s0.at[head, pair, :, pl.ds(half * DH, DH)], load_sem
            ).start()
        return carry

    lax.fori_loop(0, HEADS, load, 0)

    row = lax.broadcasted_iota(jnp.int32, (TOKENS, TOKENS), 0)
    col = lax.broadcasted_iota(jnp.int32, (TOKENS, TOKENS), 1)
    upper8 = lax.broadcasted_iota(jnp.int32, (16, 256), 0) < 8
    arrived(s0, load_sem)

    def select(head, carry):
        pick = (position(row, off_ref, head) == col).astype(F32).astype(BF16)
        sel0 = nn(pick, s0[head, 0])
        sel1 = nn(pick, s0[head, 1])
        sbuf[head, 0] = sel0[:112].astype(BF16)
        sbuf[head, 1] = sel1[:112].astype(BF16)
        s4[head] = jnp.where(upper8, sel0[112:], sel1[112:]).astype(BF16)
        return carry

    lax.fori_loop(0, HEADS, select, 0)

    pl.semaphore_wait(barrier, greetings)

    def in_copy(level, head):
        rows = ROWS[level]
        target, slot = holder(level, head)
        if level == 0:
            src = s0.at[head]
            at = upper * HALF + core * TOKENS
        elif level < 4:
            src = sbuf.at[head, :, pl.ds(FIRST[level], rows), :]
            at = inside[level] * rows
        else:
            src = s4.at[head]
        if level < 4:
            dst = ubuf.at[slot, :, pl.ds(pl.multiple_of(at, rows), rows), :]
        else:
            dst = u4.at[me]
        return src, dst, target, in_send.at[level * HEADS + head], in_recv.at[slot]

    def kv_copy(head):
        target, slot = holder(0, head)
        at = pl.ds(pl.multiple_of(core * TOKENS, TOKENS), TOKENS)
        return s0.at[head, 1], ubuf.at[slot, 1, at, :], target + 2, kv_send.at[head], kv_recv.at[slot]

    turn = lax.div(me, 2)
    for level in range(LEVELS - 1, -1, -1):

        def send_rows(i, carry):
            head = lax.rem(turn + i, HEADS)
            push(*in_copy(level, head))
            if level == 0:

                @pl.when(upper == 0)
                def _():
                    remote(*kv_copy(head))

            return carry

        lax.fori_loop(0, HEADS, send_rows, 0)

    key_i = lax.broadcasted_iota(jnp.int32, (HALF, HALF), 0)
    query_i = lax.broadcasted_iota(jnp.int32, (HALF, HALF), 1)
    causal = key_i <= query_i

    def does(level, j):
        return (level > 0) | ((level == 0) & (upper == j))

    def forward(step, carry):
        u = SLOTS - 1 - step
        level = level_of(u)
        head = head_of(u)

        @pl.when(level == 0)
        def _():
            arrived(ubuf.at[u, :, pl.ds(0, HALF), :], in_recv.at[u])

            @pl.when(upper == 1)
            def _():
                arrived(ubuf.at[u, 1, pl.ds(0, HALF), :], kv_recv.at[u])

        @pl.when((level > 0) & (level < 4))
        def _():
            arrived(ubuf.at[u], in_recv.at[u])

        @pl.when(level == 4)
        def _():
            arrived(u4, in_recv.at[u])

            def unpack(n, c):
                block = u4[pl.ds(n * 8, 8)].astype(F32)
                rows = pl.ds(pl.multiple_of(n * 64, 64), 64)
                ubuf[u, 0, rows, :] = block[:, :8, :].reshape(64, 256).astype(BF16)
                ubuf[u, 1, rows, :] = block[:, 8:, :].reshape(64, 256).astype(BF16)
                return c

            lax.fori_loop(0, 8, unpack, 0)

        for j in range(2):

            @pl.when(does(level, j))
            def _():
                keys = HALF * (j + 1)
                cols = pl.ds(j * HALF, HALF)
                q = ubuf[u, 0, cols, :DH]
                g = ubuf[u, 0, cols, DH:]
                k = ubuf[u, 1, :keys, :DH]
                v = ubuf[u, 1, :keys, DH:]
                s = nt(k, q) * SCALE
                last = jnp.where(causal, s[j * HALF :], MASKED)
                s = last if j == 0 else jnp.concatenate([s[:HALF], last], axis=0)
                m = jnp.max(s, axis=0, keepdims=True)
                e = jnp.exp(s - m)
                den = jnp.sum(e, axis=0, keepdims=True)
                ebuf[u, :keys, cols] = e
                abuf[u, :, cols] = tn(v, e.astype(BF16))
                dp = nt(v, g)
                dbuf[u, :keys, cols] = dp
                t = jnp.sum(e * dp, axis=0, keepdims=True)
                tile = jnp.concatenate([m, den, t, jnp.zeros((5, HALF), F32)], axis=0)
                stbuf[u, 2 * j] = tile[:, :128]
                stbuf[u, 2 * j + 1] = tile[:, 128:]

        @pl.when(level >= 0)
        def _():
            count = jnp.where(level == 0, 2, 4 << level)
            first = me - lax.rem(me, count)
            block = jnp.where(level == 0, 2 * upper, 0)

            def send_stats(i, c):
                push(
                    stbuf.at[u, block + lax.shift_right_logical(i, level)],
                    stin.at[level * HEADS + head],
                    first + i,
                    st_send.at[tiles_of(u) + i],
                    st_recv,
                )
                return c

            lax.fori_loop(0, count, send_stats, 0)

        return carry

    lax.fori_loop(0, SLOTS, forward, 0)

    arrived(stin, st_recv)
    lane = lax.broadcasted_iota(jnp.int32, (1, TOKENS), 1)
    spread = [None]
    stats = [stin[:HEADS]]
    for level in range(1, LEVELS):
        base = (inside[level] & ((1 << level) - 1)) * ROWS[level]
        rep = (row == base + lax.shift_right_logical(col, level)).astype(F32).astype(BF16)
        spread.append(rep)
        tiles = stin[level * HEADS : (level + 1) * HEADS].reshape(HEADS * 8, TOKENS)
        stats.append(move(tiles, rep, ((1,), (0,))).reshape(HEADS, 8, TOKENS))
    answers = [[] for _ in range(LEVELS)]
    for head in range(HEADS):
        chosen = [None] + [
            (lane & ((1 << level) - 1)) == off_ref[level, head] for level in range(1, LEVELS)
        ]
        ms = [stats[0][head, 0:1]] + [
            jnp.where(chosen[level], stats[level][head, 0:1], MASKED) for level in range(1, LEVELS)
        ]
        top = ms[0]
        for level in range(1, LEVELS):
            top = jnp.maximum(top, ms[level])
        total = jnp.zeros((1, TOKENS), F32)
        delta = jnp.zeros((1, TOKENS), F32)
        for level in range(LEVELS):
            weight = jnp.exp(ms[level] - top)
            den, t = stats[level][head, 1:2], stats[level][head, 2:3]
            if level:
                den = jnp.where(chosen[level], den, 0.0)
                t = jnp.where(chosen[level], t, 0.0)
            total = total + den * weight
            delta = delta + t * weight
        log_total = top + jnp.log(total)
        delta = delta * jnp.exp(top - log_total)
        lse_ref[head : head + 1, :] = log_total
        answer = jnp.concatenate([log_total, delta, jnp.zeros((6, TOKENS), F32)], axis=0)
        for level in range(LEVELS):
            answers[level].append(answer if level == 0 else jnp.where(chosen[level], answer, 0.0))

    def c_copy(level, head):
        n = level * HEADS + head
        target, slot = holder(level, head)
        return cout.at[n], cin.at[tiles_of(slot) + inside[level]], target, c_send.at[n], c_recv.at[slot]

    for level in range(LEVELS - 1, -1, -1):
        if level:
            packed = move(jnp.concatenate(answers[level], axis=0), spread[level], ((1,), (1,)))
            packed = packed.reshape(HEADS, 8, TOKENS)
        for head in range(HEADS):
            cout[level * HEADS + head] = packed[head] if level else answers[0][head]

        def send_answer(i, carry):
            push(*c_copy(level, lax.rem(turn + i, HEADS)))
            return carry

        lax.fori_loop(0, HEADS, send_answer, 0)

    def res_copy(u, level, i, head):
        rows = ROWS[level]
        if level < 4:
            at = i * rows if level else upper * HALF + i * rows
            src = obuf.at[u, :, pl.ds(pl.multiple_of(at, rows), rows), :]
        else:
            src = o4.at[i]
        if level == 0:
            dst, sem = r0.at[head], res_recv.at[0]
        elif level < 4:
            dst, sem = rbuf.at[head, :, pl.ds(FIRST[level], rows), :], res_recv.at[1]
        else:
            dst, sem = r4.at[head], res_recv.at[2]
        return src, dst, start[level] + i, res_send.at[tiles_of(u) + i], sem

    def res_kv_copy(u, i, head):
        src = obuf.at[u, 1, pl.ds(pl.multiple_of(i * TOKENS, TOKENS), TOKENS), :]
        return src, r0b.at[head], start[0] - 2 + i, res_kv_send.at[2 * u + i], res_recv.at[3]

    def backward(u, carry):
        level = level_of(u)
        head = head_of(u)
        base = tiles_of(u)
        for lv in range(LEVELS):

            @pl.when(level == lv)
            def _():
                arrived(cin.at[pl.ds(base, GROUP[lv])], c_recv.at[u])

        per = lax.shift_left(1, jnp.maximum(level, 0))
        origin = jnp.where(level == 0, base - 2 * upper, base)

        for j in range(2):

            @pl.when(does(level, j))
            def _():
                blocks = []
                for b in range(2 * j, 2 * j + 2):
                    blocks.append(
                        lax.fori_loop(
                            0, per, lambda i, c: c + cin[origin + b * per + i], jnp.zeros((8, TOKENS), F32)
                        )
                    )
                keys = HALF * (j + 1)
                cols = pl.ds(j * HALF, HALF)
                q = ubuf[u, 0, cols, :DH]
                g = ubuf[u, 0, cols, DH:]
                k = ubuf[u, 1, :keys, :DH]
                answer = jnp.concatenate(blocks, axis=1)
                m = jnp.concatenate([stbuf[u, 2 * j], stbuf[u, 2 * j + 1]], axis=1)[0:1]
                w = jnp.exp(m - answer[0:1])
                delta = answer[1:2]
                p = ebuf[u, :keys, cols] * w
                ds = (SCALE * p * (dbuf[u, :keys, cols] - delta)).astype(BF16)
                p = p.astype(BF16)
                o = (abuf[u, :, cols] * w).T
                dq = tn(k, ds).T
                obuf[u, 0, cols, :DH] = o.astype(BF16)
                obuf[u, 0, cols, DH:] = dq.astype(BF16)
                dk = nn(ds, q)
                dv = nn(p, g)
                if j == 0:
                    acc[:, :DH] = dk
                    acc[:, DH:] = dv
                    obuf[u, 1, :HALF, :DH] = dk.astype(BF16)
                    obuf[u, 1, :HALF, DH:] = dv.astype(BF16)
                else:
                    both = level > 0
                    obuf[u, 1, :HALF, :DH] = (dk[:HALF] + jnp.where(both, acc[:, :DH], 0.0)).astype(BF16)
                    obuf[u, 1, :HALF, DH:] = (dv[:HALF] + jnp.where(both, acc[:, DH:], 0.0)).astype(BF16)
                    obuf[u, 1, HALF:, :DH] = dk[HALF:].astype(BF16)
                    obuf[u, 1, HALF:, DH:] = dv[HALF:].astype(BF16)

        @pl.when(level == 4)
        def _():
            def pack(n, c):
                rows = pl.ds(pl.multiple_of(n * 64, 64), 64)
                lo = obuf[u, 0, rows, :].astype(F32).reshape(8, 8, 256)
                hi = obuf[u, 1, rows, :].astype(F32).reshape(8, 8, 256)
                o4[pl.ds(n * 8, 8)] = jnp.concatenate([lo, hi], axis=1).astype(BF16)
                return c

            lax.fori_loop(0, 8, pack, 0)

        for lv in range(LEVELS):

            @pl.when(level == lv)
            def _():
                def send_result(i, c):
                    push(*res_copy(u, lv, lax.rem(i + turn, GROUP[lv]), head))
                    if lv == 0:

                        @pl.when(upper == 1)
                        def _():
                            remote(*res_kv_copy(u, i, head))

                    return c

                lax.fori_loop(0, GROUP[lv], send_result, 0)

        return carry

    lax.fori_loop(0, SLOTS, backward, 0)

    arrived(r4, res_recv.at[2])
    arrived(rbuf, res_recv.at[1])
    arrived(r0, res_recv.at[0])

    @pl.when(upper == 0)
    def _():
        arrived(r0b, res_recv.at[3])

    def drain_own(head, carry):
        for level in range(LEVELS):
            src, _, target, sem, _ = in_copy(level, head)
            sent(src, target, sem)
            src, _, target, sem, _ = c_copy(level, head)
            sent(src, target, sem)

        @pl.when(upper == 0)
        def _():
            src, _, _, sem, _ = kv_copy(head)
            done(src, sem)

        return carry

    lax.fori_loop(0, HEADS, drain_own, 0)

    def drain(u, carry):
        level = level_of(u)
        for lv in range(LEVELS):

            @pl.when(level == lv)
            def _():
                def one(i, c):
                    src, _, target, sem, _ = res_copy(u, lv, i, 0)
                    sent(src, target, sem)
                    sent(stbuf.at[u, 0], target, st_send.at[tiles_of(u) + i])
                    if lv == 0:

                        @pl.when(upper == 1)
                        def _():
                            src, _, _, sem, _ = res_kv_copy(u, i, 0)
                            done(src, sem)

                    return c

                lax.fori_loop(0, GROUP[lv], one, 0)

        return carry

    lax.fori_loop(0, SLOTS, drain, 0)


def finish(off_ref, lse_ref, r0, r0b, rbuf, r4, out_ref, log_ref, dq_ref, dk_ref, dv_ref, w0, w0b, wbuf, res, log, in_sem, out_sem):
    upper = lax.rem(lax.div(lax.axis_index("seq"), 2), 2)
    row = lax.broadcasted_iota(jnp.int32, (TOKENS, TOKENS), 0)
    col = lax.broadcasted_iota(jnp.int32, (TOKENS, TOKENS), 1)

    def ins(head):
        return (
            pltpu.make_async_copy(r0.at[head], w0.at[head], in_sem.at[0, head]),
            pltpu.make_async_copy(r0b.at[head], w0b.at[head], in_sem.at[1, head]),
            pltpu.make_async_copy(rbuf.at[head], wbuf.at[head, :, pl.ds(0, 112), :], in_sem.at[2, head]),
            pltpu.make_async_copy(r4.at[head], wbuf.at[head, 0, pl.ds(112, 16), :], in_sem.at[3, head]),
            pltpu.make_async_copy(r4.at[head], wbuf.at[head, 1, pl.ds(112, 16), :], in_sem.at[4, head]),
        )

    def outs(head):
        lanes = pl.ds(head * DH, DH)
        return [
            pltpu.make_async_copy(res.at[n, head], ref.at[:, lanes], out_sem.at[n, head])
            for n, ref in enumerate((out_ref, dq_ref, dk_ref, dv_ref))
        ]

    for head in range(HEADS):
        for copy in ins(head):
            copy.start()
    log_in = pltpu.make_async_copy(lse_ref, log, in_sem.at[5, 0])
    log_out = pltpu.make_async_copy(log, log_ref, out_sem.at[4, 0])
    log_in.start()
    puts = []
    for head in range(HEADS):
        hit = position(col, off_ref, head) == row
        puts.append((
            (hit & (col < 120)).astype(F32).astype(BF16),
            (hit & ((col < 112) | (col >= 120))).astype(F32).astype(BF16),
        ))
    log_in.wait()
    log_out.start()
    for head in range(HEADS):
        for copy in ins(head):
            copy.wait()
        all0 = w0[head, 0].astype(F32) + nn(puts[head][0], wbuf[head, 0])
        all1 = w0[head, 1].astype(F32) + nn(puts[head][1], wbuf[head, 1])
        all1 = all1 + jnp.where(upper == 0, w0b[head].astype(F32), 0.0)
        res[0, head] = all0[:, :DH].astype(BF16)
        res[1, head] = all0[:, DH:].astype(BF16)
        res[2, head] = all1[:, :DH].astype(BF16)
        res[3, head] = all1[:, DH:].astype(BF16)
        for copy in outs(head):
            copy.start()
    for head in range(HEADS):
        for copy in outs(head):
            copy.wait()
    log_out.wait()


def on_device(query_in, key_in, value_in, grad_out, offsets):
    hbm = pl.BlockSpec(memory_space=pl.ANY)
    smem = pl.BlockSpec(memory_space=pltpu.SMEM)
    parts = pl.pallas_call(
        kernel,
        out_shape=(
            jax.ShapeDtypeStruct((HEADS, TOKENS), F32),
            jax.ShapeDtypeStruct((HEADS, 2, TOKENS, 256), BF16),
            jax.ShapeDtypeStruct((HEADS, TOKENS, 256), BF16),
            jax.ShapeDtypeStruct((HEADS, 2, 112, 256), BF16),
            jax.ShapeDtypeStruct((HEADS, 16, 256), BF16),
        ),
        in_specs=[hbm] * 4 + [smem],
        out_specs=(pl.BlockSpec(memory_space=pltpu.VMEM),) + (hbm,) * 4,
        scratch_shapes=[
            pltpu.VMEM((HEADS, 2, TOKENS, 256), BF16),
            pltpu.VMEM((HEADS, 2, 112, 256), BF16),
            pltpu.VMEM((HEADS, 16, 256), BF16),
            pltpu.VMEM((SLOTS, 2, SUB, 256), BF16),
            pltpu.VMEM((SEQ_DEVICES, 16, 256), BF16),
            pltpu.VMEM((SLOTS, SUB, SUB), F32),
            pltpu.VMEM((SLOTS, SUB, SUB), F32),
            pltpu.VMEM((SLOTS, DH, SUB), F32),
            pltpu.VMEM((SLOTS, 4, 8, 128), F32),
            pltpu.VMEM((LEVELS * HEADS, 8, 128), F32),
            pltpu.VMEM((LEVELS * HEADS, 8, 128), F32),
            pltpu.VMEM((TILES, 8, 128), F32),
            pltpu.VMEM((HALF, 256), F32),
            pltpu.VMEM((SLOTS, 2, SUB, 256), BF16),
            pltpu.VMEM((SEQ_DEVICES, 16, 256), BF16),
            pltpu.SemaphoreType.DMA,
            pltpu.SemaphoreType.DMA((LEVELS * HEADS,)),
            pltpu.SemaphoreType.DMA((HEADS,)),
            pltpu.SemaphoreType.DMA((SLOTS,)),
            pltpu.SemaphoreType.DMA((3,)),
            pltpu.SemaphoreType.DMA((TILES,)),
            pltpu.SemaphoreType.DMA,
            pltpu.SemaphoreType.DMA((LEVELS * HEADS,)),
            pltpu.SemaphoreType.DMA((SLOTS,)),
            pltpu.SemaphoreType.DMA((TILES,)),
            pltpu.SemaphoreType.DMA((6,)),
            pltpu.SemaphoreType.DMA((4,)),
        ],
        compiler_params=pltpu.CompilerParams(
            collective_id=0, has_side_effects=True, vmem_limit_bytes=60 * 1024 * 1024
        ),
    )(query_in, key_in, value_in, grad_out, offsets)
    flat = jax.ShapeDtypeStruct((TOKENS, HEADS * DH), BF16)
    return pl.pallas_call(
        finish,
        out_shape=(flat, jax.ShapeDtypeStruct((HEADS, TOKENS), F32), flat, flat, flat),
        in_specs=[smem] + [hbm] * 5,
        out_specs=(hbm,) * 5,
        scratch_shapes=[
            pltpu.VMEM((HEADS, 2, TOKENS, 256), BF16),
            pltpu.VMEM((HEADS, TOKENS, 256), BF16),
            pltpu.VMEM((HEADS, 2, TOKENS, 256), BF16),
            pltpu.VMEM((4, HEADS, TOKENS, DH), BF16),
            pltpu.VMEM((HEADS, TOKENS), F32),
            pltpu.SemaphoreType.DMA((6, HEADS)),
            pltpu.SemaphoreType.DMA((5, HEADS)),
        ],
        compiler_params=pltpu.CompilerParams(vmem_limit_bytes=60 * 1024 * 1024),
    )(offsets, *parts)


def solution(mesh):
    return jax.shard_map(
        on_device,
        mesh=mesh,
        in_specs=(P("seq", "head"),) * 4 + (P(None, "head"),),
        out_specs=(P("seq", "head"), P("head", "seq")) + (P("seq", "head"),) * 3,
        check_vma=False,
    )
```

```python
import jax
import jax.numpy as jnp
from jax import lax
from jax.experimental import pallas as pl
from jax.experimental.pallas import tpu as pltpu
from jax.sharding import PartitionSpec as P

MESH = pl.DeviceIdType.MESH
F32 = jnp.float32
BF16 = jnp.bfloat16

SEQ_DEVICES = 64
HEADS = 5
LEVELS = 5
DH = 128
TOKENS = 128
SUB = 512
HALF = 256
SCALE = DH ** (-0.5)
MASKED = -1e30

GROUP = [2] + [4 << level for level in range(1, LEVELS)]
ROWS = [TOKENS >> level for level in range(LEVELS)]
PLACE = [
    None,
    [0, 2, 3, 4, 5],
    [0, 6, 7, 8, 9],
    [5, 15, 17, 28, 31],
    [1, 12, 33, 45, 52],
]
SLOTS = 5
FIRST = [0, 0, 64, 96, 112]
TILES = 2 * 3 + 8 + 64


def dot(a, b, dims):
    return lax.dot_general(a, b, (dims, ((), ())), preferred_element_type=F32)


def nn(a, b):
    return dot(a, b, ((1,), (0,)))


def nt(a, b):
    return dot(a, b, ((1,), (1,)))


def tn(a, b):
    return dot(a, b, ((0,), (0,)))


def move(tiles, rep, dims):
    rows = tiles.shape[0]
    high = tiles.astype(BF16).astype(F32)
    mid = (tiles - high).astype(BF16).astype(F32)
    low = tiles - high - mid
    out = dot(jnp.concatenate([high, mid, low], axis=0).astype(BF16), rep, dims)
    return (out[2 * rows :] + out[rows : 2 * rows]) + out[:rows]


def position(index, off_ref, head):
    return jnp.where(
        index < 64,
        2 * index + off_ref[1, head],
        jnp.where(
            index < 96,
            4 * (index - 64) + off_ref[2, head],
            jnp.where(
                index < 112,
                8 * (index - 96) + off_ref[3, head],
                16 * ((index - 112) & 7) + off_ref[4, head],
            ),
        ),
    )


def kernel(
    q_ref, k_ref, v_ref, g_ref, off_ref,
    lse_ref, r0, r0b, rbuf, r4,
    s0, sbuf, s4, ubuf, u4, ebuf, dbuf, abuf, stbuf, stin, cout, cin, acc, obuf, o4,
    load_sem, in_send, kv_send, in_recv, kv_recv, st_send, st_recv, c_send, c_recv, res_send, res_kv_send, res_recv,
):
    me = lax.axis_index("seq")
    inside = [lax.rem(me, g) for g in GROUP]
    start = [me - i for i in inside]
    core = inside[0]
    upper = lax.rem(lax.div(me, 2), 2)

    level3 = jnp.int32(-1)
    head3 = jnp.int32(0)
    level4 = jnp.int32(-1)
    head4 = jnp.int32(0)
    for level in range(1, LEVELS):
        for head in range(HEADS):
            held = inside[level] == PLACE[level][head]
            if level == 1:
                level3 = jnp.where(held, level, level3)
                head3 = jnp.where(held, head, head3)
            else:
                level4 = jnp.where(held, level, level4)
                head4 = jnp.where(held, head, head4)

    def level_of(u):
        local = jnp.where((u == 2) & (core == 1), -1, 0)
        return jnp.where(u < 3, local, jnp.where(u == 3, level3, level4))

    def head_of(u):
        local = jnp.where(u == 2, 4, u + 2 * core)
        return jnp.where(u < 3, local, jnp.where(u == 3, head3, head4))

    def tiles_of(u):
        return jnp.where(u < 3, 2 * u, jnp.where(u == 3, 6, 14))

    def holder(level, head):
        if level == 0:
            return start[0] + (lax.div(head, 2) & 1), (head & 1) + 2 * lax.div(head, 4)
        place = jnp.int32(0)
        for h in range(HEADS):
            place = jnp.where(head == h, PLACE[level][h], place)
        return start[level] + place, 3 if level == 1 else 4

    def remote(src, dst, target, send_sem, recv_sem):
        pltpu.make_async_remote_copy(
            src_ref=src, dst_ref=dst, send_sem=send_sem, recv_sem=recv_sem,
            device_id={"seq": target}, device_id_type=MESH,
        ).start()

    def push(src, dst, target, send_sem, recv_sem):
        @pl.when(target != me)
        def _():
            remote(src, dst, target, send_sem, recv_sem)

        @pl.when(target == me)
        def _():
            pltpu.make_async_copy(src, dst, recv_sem).start()

    def done(src, send_sem):
        pltpu.make_async_copy(src, src, send_sem).wait()

    def sent(src, target, send_sem):
        @pl.when(target != me)
        def _():
            done(src, send_sem)

    arrived = done

    barrier = pltpu.get_barrier_semaphore()

    def greet(target):
        pl.semaphore_signal(barrier, inc=1, device_id={"seq": target}, device_id_type=MESH)

    def greet_members(count):
        first = me - lax.rem(me, count)

        def one(i, carry):
            greet(first + lax.rem(me - first + i, count))
            return carry

        lax.fori_loop(1, count, one, 0)

    other = me - 2 * upper - core + 2 - 2 * upper
    greet(start[0] + 1 - core)
    greet(other)
    greet(other + 1)
    greetings = jnp.int32(3)
    for level in range(LEVELS - 1, 0, -1):

        def greet_holder(head, count):
            target, _ = holder(level, head)

            @pl.when(target != me)
            def _():
                greet(target)

            return count + jnp.where(target != me, 1, 0)

        greetings = lax.fori_loop(0, HEADS, greet_holder, greetings)
    for level in (level4, level3):

        @pl.when(level > 0)
        def _():
            greet_members(4 << level)

        greetings = greetings + jnp.where(level > 0, lax.shift_left(4, jnp.maximum(level, 0)) - 1, 0)

    def load(head, carry):
        lanes = pl.ds(pl.multiple_of(head * DH, DH), DH)
        for pair, half, ref in ((0, 0, q_ref), (0, 1, g_ref), (1, 0, k_ref), (1, 1, v_ref)):
            pltpu.make_async_copy(
                ref.at[:, lanes], s0.at[head, pair, :, pl.ds(half * DH, DH)], load_sem
            ).start()
        return carry

    lax.fori_loop(0, HEADS, load, 0)

    row = lax.broadcasted_iota(jnp.int32, (TOKENS, TOKENS), 0)
    col = lax.broadcasted_iota(jnp.int32, (TOKENS, TOKENS), 1)
    upper8 = lax.broadcasted_iota(jnp.int32, (16, 256), 0) < 8
    arrived(s0, load_sem)

    def select(head, carry):
        pick = (position(row, off_ref, head) == col).astype(F32).astype(BF16)
        sel0 = nn(pick, s0[head, 0])
        sel1 = nn(pick, s0[head, 1])
        sbuf[head, 0] = sel0[:112].astype(BF16)
        sbuf[head, 1] = sel1[:112].astype(BF16)
        s4[head] = jnp.where(upper8, sel0[112:], sel1[112:]).astype(BF16)
        return carry

    lax.fori_loop(0, HEADS, select, 0)

    pl.semaphore_wait(barrier, greetings)

    def in_copy(level, head):
        rows = ROWS[level]
        target, slot = holder(level, head)
        if level == 0:
            src = s0.at[head]
            at = upper * HALF + core * TOKENS
        elif level < 4:
            src = sbuf.at[head, :, pl.ds(FIRST[level], rows), :]
            at = inside[level] * rows
        else:
            src = s4.at[head]
        if level < 4:
            dst = ubuf.at[slot, :, pl.ds(pl.multiple_of(at, rows), rows), :]
        else:
            dst = u4.at[me]
        return src, dst, target, in_send.at[level * HEADS + head], in_recv.at[slot]

    def kv_copy(head):
        target, slot = holder(0, head)
        at = pl.ds(pl.multiple_of(core * TOKENS, TOKENS), TOKENS)
        return s0.at[head, 1], ubuf.at[slot, 1, at, :], target + 2, kv_send.at[head], kv_recv.at[slot]

    turn = me
    for level in range(LEVELS - 1, -1, -1):

        def send_rows(i, carry):
            head = lax.rem(turn + i, HEADS)
            push(*in_copy(level, head))
            if level == 0:

                @pl.when(upper == 0)
                def _():
                    remote(*kv_copy(head))

            return carry

        lax.fori_loop(0, HEADS, send_rows, 0)

    key_i = lax.broadcasted_iota(jnp.int32, (HALF, HALF), 0)
    query_i = lax.broadcasted_iota(jnp.int32, (HALF, HALF), 1)
    causal = key_i <= query_i

    def does(level, j):
        return (level > 0) | ((level == 0) & (upper == j))

    def forward(step, carry):
        u = SLOTS - 1 - step
        level = level_of(u)
        head = head_of(u)

        @pl.when(level == 0)
        def _():
            arrived(ubuf.at[u, :, pl.ds(0, HALF), :], in_recv.at[u])

            @pl.when(upper == 1)
            def _():
                arrived(ubuf.at[u, 1, pl.ds(0, HALF), :], kv_recv.at[u])

        @pl.when((level > 0) & (level < 4))
        def _():
            arrived(ubuf.at[u], in_recv.at[u])

        @pl.when(level == 4)
        def _():
            arrived(u4, in_recv.at[u])

            def unpack(n, c):
                block = u4[pl.ds(n * 8, 8)].astype(F32)
                rows = pl.ds(pl.multiple_of(n * 64, 64), 64)
                ubuf[u, 0, rows, :] = block[:, :8, :].reshape(64, 256).astype(BF16)
                ubuf[u, 1, rows, :] = block[:, 8:, :].reshape(64, 256).astype(BF16)
                return c

            lax.fori_loop(0, 8, unpack, 0)

        for j in range(2):

            @pl.when(does(level, j))
            def _():
                keys = HALF * (j + 1)
                cols = pl.ds(j * HALF, HALF)
                q = ubuf[u, 0, cols, :DH]
                g = ubuf[u, 0, cols, DH:]
                k = ubuf[u, 1, :keys, :DH]
                v = ubuf[u, 1, :keys, DH:]
                s = nt(k, q) * SCALE
                last = jnp.where(causal, s[j * HALF :], MASKED)
                s = last if j == 0 else jnp.concatenate([s[:HALF], last], axis=0)
                m = jnp.max(s, axis=0, keepdims=True)
                e = jnp.exp(s - m)
                den = jnp.sum(e, axis=0, keepdims=True)
                ebuf[u, :keys, cols] = e
                abuf[u, :, cols] = tn(v, e.astype(BF16))
                dp = nt(v, g)
                dbuf[u, :keys, cols] = dp
                t = jnp.sum(e * dp, axis=0, keepdims=True)
                tile = jnp.concatenate([m, den, t, jnp.zeros((5, HALF), F32)], axis=0)
                stbuf[u, 2 * j] = tile[:, :128]
                stbuf[u, 2 * j + 1] = tile[:, 128:]

        @pl.when(level >= 0)
        def _():
            count = jnp.where(level == 0, 2, 4 << level)
            first = me - lax.rem(me, count)
            block = jnp.where(level == 0, 2 * upper, 0)

            def send_stats(i, c):
                push(
                    stbuf.at[u, block + lax.shift_right_logical(i, level)],
                    stin.at[level * HEADS + head],
                    first + i,
                    st_send.at[tiles_of(u) + i],
                    st_recv,
                )
                return c

            lax.fori_loop(0, count, send_stats, 0)

        return carry

    lax.fori_loop(0, SLOTS, forward, 0)

    arrived(stin, st_recv)
    lane = lax.broadcasted_iota(jnp.int32, (1, TOKENS), 1)
    spread = [None]
    stats = [stin[:HEADS]]
    for level in range(1, LEVELS):
        base = (inside[level] & ((1 << level) - 1)) * ROWS[level]
        rep = (row == base + lax.shift_right_logical(col, level)).astype(F32).astype(BF16)
        spread.append(rep)
        tiles = stin[level * HEADS : (level + 1) * HEADS].reshape(HEADS * 8, TOKENS)
        stats.append(move(tiles, rep, ((1,), (0,))).reshape(HEADS, 8, TOKENS))
    answers = [[] for _ in range(LEVELS)]
    for head in range(HEADS):
        chosen = [None] + [
            (lane & ((1 << level) - 1)) == off_ref[level, head] for level in range(1, LEVELS)
        ]
        ms = [stats[0][head, 0:1]] + [
            jnp.where(chosen[level], stats[level][head, 0:1], MASKED) for level in range(1, LEVELS)
        ]
        top = ms[0]
        for level in range(1, LEVELS):
            top = jnp.maximum(top, ms[level])
        total = jnp.zeros((1, TOKENS), F32)
        delta = jnp.zeros((1, TOKENS), F32)
        for level in range(LEVELS):
            weight = jnp.exp(ms[level] - top)
            den, t = stats[level][head, 1:2], stats[level][head, 2:3]
            if level:
                den = jnp.where(chosen[level], den, 0.0)
                t = jnp.where(chosen[level], t, 0.0)
            total = total + den * weight
            delta = delta + t * weight
        log_total = top + jnp.log(total)
        delta = delta * jnp.exp(top - log_total)
        lse_ref[head : head + 1, :] = log_total
        answer = jnp.concatenate([log_total, delta, jnp.zeros((6, TOKENS), F32)], axis=0)
        for level in range(LEVELS):
            answers[level].append(answer if level == 0 else jnp.where(chosen[level], answer, 0.0))

    def c_copy(level, head):
        n = level * HEADS + head
        target, slot = holder(level, head)
        return cout.at[n], cin.at[tiles_of(slot) + inside[level]], target, c_send.at[n], c_recv.at[slot]

    for level in range(LEVELS - 1, -1, -1):
        if level:
            packed = move(jnp.concatenate(answers[level], axis=0), spread[level], ((1,), (1,)))
            packed = packed.reshape(HEADS, 8, TOKENS)
        for head in range(HEADS):
            cout[level * HEADS + head] = packed[head] if level else answers[0][head]

        def send_answer(i, carry):
            push(*c_copy(level, lax.rem(turn + i, HEADS)))
            return carry

        lax.fori_loop(0, HEADS, send_answer, 0)

    def res_copy(u, level, i, head):
        rows = ROWS[level]
        if level < 4:
            at = i * rows if level else upper * HALF + i * rows
            src = obuf.at[u, :, pl.ds(pl.multiple_of(at, rows), rows), :]
        else:
            src = o4.at[i]
        if level == 0:
            dst, sem = r0.at[head], res_recv.at[0]
        elif level < 4:
            dst, sem = rbuf.at[head, :, pl.ds(FIRST[level], rows), :], res_recv.at[1]
        else:
            dst, sem = r4.at[head], res_recv.at[2]
        return src, dst, start[level] + i, res_send.at[tiles_of(u) + i], sem

    def res_kv_copy(u, i, head):
        src = obuf.at[u, 1, pl.ds(pl.multiple_of(i * TOKENS, TOKENS), TOKENS), :]
        return src, r0b.at[head], start[0] - 2 + i, res_kv_send.at[2 * u + i], res_recv.at[3]

    def backward(u, carry):
        level = level_of(u)
        head = head_of(u)
        base = tiles_of(u)
        for lv in range(LEVELS):

            @pl.when(level == lv)
            def _():
                arrived(cin.at[pl.ds(base, GROUP[lv])], c_recv.at[u])

        per = lax.shift_left(1, jnp.maximum(level, 0))
        origin = jnp.where(level == 0, base - 2 * upper, base)

        for j in range(2):

            @pl.when(does(level, j))
            def _():
                blocks = []
                for b in range(2 * j, 2 * j + 2):
                    blocks.append(
                        lax.fori_loop(
                            0, per, lambda i, c: c + cin[origin + b * per + i], jnp.zeros((8, TOKENS), F32)
                        )
                    )
                keys = HALF * (j + 1)
                cols = pl.ds(j * HALF, HALF)
                q = ubuf[u, 0, cols, :DH]
                g = ubuf[u, 0, cols, DH:]
                k = ubuf[u, 1, :keys, :DH]
                answer = jnp.concatenate(blocks, axis=1)
                m = jnp.concatenate([stbuf[u, 2 * j], stbuf[u, 2 * j + 1]], axis=1)[0:1]
                w = jnp.exp(m - answer[0:1])
                delta = answer[1:2]
                p = ebuf[u, :keys, cols] * w
                ds = (SCALE * p * (dbuf[u, :keys, cols] - delta)).astype(BF16)
                p = p.astype(BF16)
                o = (abuf[u, :, cols] * w).T
                dq = tn(k, ds).T
                obuf[u, 0, cols, :DH] = o.astype(BF16)
                obuf[u, 0, cols, DH:] = dq.astype(BF16)
                dk = nn(ds, q)
                dv = nn(p, g)
                if j == 0:
                    acc[:, :DH] = dk
                    acc[:, DH:] = dv
                    obuf[u, 1, :HALF, :DH] = dk.astype(BF16)
                    obuf[u, 1, :HALF, DH:] = dv.astype(BF16)
                else:
                    both = level > 0
                    obuf[u, 1, :HALF, :DH] = (dk[:HALF] + jnp.where(both, acc[:, :DH], 0.0)).astype(BF16)
                    obuf[u, 1, :HALF, DH:] = (dv[:HALF] + jnp.where(both, acc[:, DH:], 0.0)).astype(BF16)
                    obuf[u, 1, HALF:, :DH] = dk[HALF:].astype(BF16)
                    obuf[u, 1, HALF:, DH:] = dv[HALF:].astype(BF16)

        @pl.when(level == 4)
        def _():
            def pack(n, c):
                rows = pl.ds(pl.multiple_of(n * 64, 64), 64)
                lo = obuf[u, 0, rows, :].astype(F32).reshape(8, 8, 256)
                hi = obuf[u, 1, rows, :].astype(F32).reshape(8, 8, 256)
                o4[pl.ds(n * 8, 8)] = jnp.concatenate([lo, hi], axis=1).astype(BF16)
                return c

            lax.fori_loop(0, 8, pack, 0)

        for lv in range(LEVELS):

            @pl.when(level == lv)
            def _():
                def send_result(i, c):
                    push(*res_copy(u, lv, lax.rem(i + turn, GROUP[lv]), head))
                    if lv == 0:

                        @pl.when(upper == 1)
                        def _():
                            remote(*res_kv_copy(u, i, head))

                    return c

                lax.fori_loop(0, GROUP[lv], send_result, 0)

        return carry

    lax.fori_loop(0, SLOTS, backward, 0)

    arrived(r4, res_recv.at[2])
    arrived(rbuf, res_recv.at[1])
    arrived(r0, res_recv.at[0])

    @pl.when(upper == 0)
    def _():
        arrived(r0b, res_recv.at[3])

    def drain_own(head, carry):
        for level in range(LEVELS):
            src, _, target, sem, _ = in_copy(level, head)
            sent(src, target, sem)
            src, _, target, sem, _ = c_copy(level, head)
            sent(src, target, sem)

        @pl.when(upper == 0)
        def _():
            src, _, _, sem, _ = kv_copy(head)
            done(src, sem)

        return carry

    lax.fori_loop(0, HEADS, drain_own, 0)

    def drain(u, carry):
        level = level_of(u)
        for lv in range(LEVELS):

            @pl.when(level == lv)
            def _():
                def one(i, c):
                    src, _, target, sem, _ = res_copy(u, lv, i, 0)
                    sent(src, target, sem)
                    sent(stbuf.at[u, 0], target, st_send.at[tiles_of(u) + i])
                    if lv == 0:

                        @pl.when(upper == 1)
                        def _():
                            src, _, _, sem, _ = res_kv_copy(u, i, 0)
                            done(src, sem)

                    return c

                lax.fori_loop(0, GROUP[lv], one, 0)

        return carry

    lax.fori_loop(0, SLOTS, drain, 0)


def finish(off_ref, lse_ref, r0, r0b, rbuf, r4, out_ref, log_ref, dq_ref, dk_ref, dv_ref, w0, w0b, wbuf, res, log, in_sem, out_sem):
    upper = lax.rem(lax.div(lax.axis_index("seq"), 2), 2)
    row = lax.broadcasted_iota(jnp.int32, (TOKENS, TOKENS), 0)
    col = lax.broadcasted_iota(jnp.int32, (TOKENS, TOKENS), 1)

    def ins(head):
        return (
            pltpu.make_async_copy(r0.at[head], w0.at[head], in_sem.at[0, head]),
            pltpu.make_async_copy(r0b.at[head], w0b.at[head], in_sem.at[1, head]),
            pltpu.make_async_copy(rbuf.at[head], wbuf.at[head, :, pl.ds(0, 112), :], in_sem.at[2, head]),
            pltpu.make_async_copy(r4.at[head], wbuf.at[head, 0, pl.ds(112, 16), :], in_sem.at[3, head]),
            pltpu.make_async_copy(r4.at[head], wbuf.at[head, 1, pl.ds(112, 16), :], in_sem.at[4, head]),
        )

    def outs(head):
        lanes = pl.ds(head * DH, DH)
        return [
            pltpu.make_async_copy(res.at[n, head], ref.at[:, lanes], out_sem.at[n, head])
            for n, ref in enumerate((out_ref, dq_ref, dk_ref, dv_ref))
        ]

    for head in range(HEADS):
        for copy in ins(head):
            copy.start()
    log_in = pltpu.make_async_copy(lse_ref, log, in_sem.at[5, 0])
    log_out = pltpu.make_async_copy(log, log_ref, out_sem.at[4, 0])
    log_in.start()
    puts = []
    for head in range(HEADS):
        hit = position(col, off_ref, head) == row
        puts.append((
            (hit & (col < 120)).astype(F32).astype(BF16),
            (hit & ((col < 112) | (col >= 120))).astype(F32).astype(BF16),
        ))
    log_in.wait()
    log_out.start()
    for head in range(HEADS):
        for copy in ins(head):
            copy.wait()
        all0 = w0[head, 0].astype(F32) + nn(puts[head][0], wbuf[head, 0])
        all1 = w0[head, 1].astype(F32) + nn(puts[head][1], wbuf[head, 1])
        all1 = all1 + jnp.where(upper == 0, w0b[head].astype(F32), 0.0)
        res[0, head] = all0[:, :DH].astype(BF16)
        res[1, head] = all0[:, DH:].astype(BF16)
        res[2, head] = all1[:, :DH].astype(BF16)
        res[3, head] = all1[:, DH:].astype(BF16)
        for copy in outs(head):
            copy.start()
    for head in range(HEADS):
        for copy in outs(head):
            copy.wait()
    log_out.wait()


def on_device(query_in, key_in, value_in, grad_out, offsets):
    hbm = pl.BlockSpec(memory_space=pl.ANY)
    smem = pl.BlockSpec(memory_space=pltpu.SMEM)
    parts = pl.pallas_call(
        kernel,
        out_shape=(
            jax.ShapeDtypeStruct((HEADS, TOKENS), F32),
            jax.ShapeDtypeStruct((HEADS, 2, TOKENS, 256), BF16),
            jax.ShapeDtypeStruct((HEADS, TOKENS, 256), BF16),
            jax.ShapeDtypeStruct((HEADS, 2, 112, 256), BF16),
            jax.ShapeDtypeStruct((HEADS, 16, 256), BF16),
        ),
        in_specs=[hbm] * 4 + [smem],
        out_specs=(pl.BlockSpec(memory_space=pltpu.VMEM),) + (hbm,) * 4,
        scratch_shapes=[
            pltpu.VMEM((HEADS, 2, TOKENS, 256), BF16),
            pltpu.VMEM((HEADS, 2, 112, 256), BF16),
            pltpu.VMEM((HEADS, 16, 256), BF16),
            pltpu.VMEM((SLOTS, 2, SUB, 256), BF16),
            pltpu.VMEM((SEQ_DEVICES, 16, 256), BF16),
            pltpu.VMEM((SLOTS, SUB, SUB), F32),
            pltpu.VMEM((SLOTS, SUB, SUB), F32),
            pltpu.VMEM((SLOTS, DH, SUB), F32),
            pltpu.VMEM((SLOTS, 4, 8, 128), F32),
            pltpu.VMEM((LEVELS * HEADS, 8, 128), F32),
            pltpu.VMEM((LEVELS * HEADS, 8, 128), F32),
            pltpu.VMEM((TILES, 8, 128), F32),
            pltpu.VMEM((HALF, 256), F32),
            pltpu.VMEM((SLOTS, 2, SUB, 256), BF16),
            pltpu.VMEM((SEQ_DEVICES, 16, 256), BF16),
            pltpu.SemaphoreType.DMA,
            pltpu.SemaphoreType.DMA((LEVELS * HEADS,)),
            pltpu.SemaphoreType.DMA((HEADS,)),
            pltpu.SemaphoreType.DMA((SLOTS,)),
            pltpu.SemaphoreType.DMA((3,)),
            pltpu.SemaphoreType.DMA((TILES,)),
            pltpu.SemaphoreType.DMA,
            pltpu.SemaphoreType.DMA((LEVELS * HEADS,)),
            pltpu.SemaphoreType.DMA((SLOTS,)),
            pltpu.SemaphoreType.DMA((TILES,)),
            pltpu.SemaphoreType.DMA((6,)),
            pltpu.SemaphoreType.DMA((4,)),
        ],
        compiler_params=pltpu.CompilerParams(
            collective_id=0, has_side_effects=True, vmem_limit_bytes=60 * 1024 * 1024
        ),
    )(query_in, key_in, value_in, grad_out, offsets)
    flat = jax.ShapeDtypeStruct((TOKENS, HEADS * DH), BF16)
    return pl.pallas_call(
        finish,
        out_shape=(flat, jax.ShapeDtypeStruct((HEADS, TOKENS), F32), flat, flat, flat),
        in_specs=[smem] + [hbm] * 5,
        out_specs=(hbm,) * 5,
        scratch_shapes=[
            pltpu.VMEM((HEADS, 2, TOKENS, 256), BF16),
            pltpu.VMEM((HEADS, TOKENS, 256), BF16),
            pltpu.VMEM((HEADS, 2, TOKENS, 256), BF16),
            pltpu.VMEM((4, HEADS, TOKENS, DH), BF16),
            pltpu.VMEM((HEADS, TOKENS), F32),
            pltpu.SemaphoreType.DMA((6, HEADS)),
            pltpu.SemaphoreType.DMA((5, HEADS)),
        ],
        compiler_params=pltpu.CompilerParams(vmem_limit_bytes=60 * 1024 * 1024),
    )(offsets, *parts)


def solution(mesh):
    return jax.shard_map(
        on_device,
        mesh=mesh,
        in_specs=(P("seq", "head"),) * 4 + (P(None, "head"),),
        out_specs=(P("seq", "head"), P("head", "seq")) + (P("seq", "head"),) * 3,
        check_vma=False,
    )
```

```python
import jax
import jax.numpy as jnp
from jax import lax
from jax.experimental import pallas as pl
from jax.experimental.pallas import tpu as pltpu
from jax.sharding import PartitionSpec as P

MESH = pl.DeviceIdType.MESH
F32 = jnp.float32
BF16 = jnp.bfloat16

SEQ_DEVICES = 64
HEADS = 5
LEVELS = 5
DH = 128
TOKENS = 128
SUB = 512
HALF = 256
SCALE = DH ** (-0.5)
MASKED = -1e30

GROUP = [2] + [4 << level for level in range(1, LEVELS)]
ROWS = [TOKENS >> level for level in range(LEVELS)]
PLACE = [
    None,
    [0, 2, 3, 4, 5],
    [0, 6, 7, 8, 9],
    [5, 15, 17, 28, 31],
    [1, 12, 33, 45, 52],
]
SLOTS = 5
FIRST = [0, 0, 64, 96, 112]
TILES = 2 * 3 + 8 + 64


def dot(a, b, dims):
    return lax.dot_general(a, b, (dims, ((), ())), preferred_element_type=F32)


def nn(a, b):
    return dot(a, b, ((1,), (0,)))


def nt(a, b):
    return dot(a, b, ((1,), (1,)))


def tn(a, b):
    return dot(a, b, ((0,), (0,)))


def move(tiles, rep, dims):
    rows = tiles.shape[0]
    high = tiles.astype(BF16).astype(F32)
    mid = (tiles - high).astype(BF16).astype(F32)
    low = tiles - high - mid
    out = dot(jnp.concatenate([high, mid, low], axis=0).astype(BF16), rep, dims)
    return (out[2 * rows :] + out[rows : 2 * rows]) + out[:rows]


def position(index, off_ref, head):
    return jnp.where(
        index < 64,
        2 * index + off_ref[1, head],
        jnp.where(
            index < 96,
            4 * (index - 64) + off_ref[2, head],
            jnp.where(
                index < 112,
                8 * (index - 96) + off_ref[3, head],
                16 * ((index - 112) & 7) + off_ref[4, head],
            ),
        ),
    )


def kernel(
    q_ref, k_ref, v_ref, g_ref, off_ref,
    lse_ref, r0, r0b, rbuf, r4,
    s0, sbuf, s4, ubuf, u4, ebuf, dbuf, abuf, stbuf, stin, cout, cin, acc, obuf, o4,
    load_sem, in_send, kv_send, in_recv, kv_recv, st_send, st_recv, c_send, c_recv, res_send, res_kv_send, res_recv,
):
    me = lax.axis_index("seq")
    inside = [lax.rem(me, g) for g in GROUP]
    start = [me - i for i in inside]
    core = inside[0]
    upper = lax.rem(lax.div(me, 2), 2)

    level3 = jnp.int32(-1)
    head3 = jnp.int32(0)
    level4 = jnp.int32(-1)
    head4 = jnp.int32(0)
    for level in range(1, LEVELS):
        for head in range(HEADS):
            held = inside[level] == PLACE[level][head]
            if level == 1:
                level3 = jnp.where(held, level, level3)
                head3 = jnp.where(held, head, head3)
            else:
                level4 = jnp.where(held, level, level4)
                head4 = jnp.where(held, head, head4)

    def level_of(u):
        local = jnp.where((u == 2) & (core == 1), -1, 0)
        return jnp.where(u < 3, local, jnp.where(u == 3, level3, level4))

    def head_of(u):
        local = jnp.where(u == 2, 4, u + 2 * core)
        return jnp.where(u < 3, local, jnp.where(u == 3, head3, head4))

    def tiles_of(u):
        return jnp.where(u < 3, 2 * u, jnp.where(u == 3, 6, 14))

    def holder(level, head):
        if level == 0:
            return start[0] + (lax.div(head, 2) & 1), (head & 1) + 2 * lax.div(head, 4)
        place = jnp.int32(0)
        for h in range(HEADS):
            place = jnp.where(head == h, PLACE[level][h], place)
        return start[level] + place, 3 if level == 1 else 4

    def remote(src, dst, target, send_sem, recv_sem):
        pltpu.make_async_remote_copy(
            src_ref=src, dst_ref=dst, send_sem=send_sem, recv_sem=recv_sem,
            device_id={"seq": target}, device_id_type=MESH,
        ).start()

    def push(src, dst, target, send_sem, recv_sem):
        @pl.when(target != me)
        def _():
            remote(src, dst, target, send_sem, recv_sem)

        @pl.when(target == me)
        def _():
            pltpu.make_async_copy(src, dst, recv_sem).start()

    def done(src, send_sem):
        pltpu.make_async_copy(src, src, send_sem).wait()

    def sent(src, target, send_sem):
        @pl.when(target != me)
        def _():
            done(src, send_sem)

    arrived = done

    barrier = pltpu.get_barrier_semaphore()

    def greet(target):
        pl.semaphore_signal(barrier, inc=1, device_id={"seq": target}, device_id_type=MESH)

    def greet_members(count):
        first = me - lax.rem(me, count)

        def one(i, carry):
            greet(first + lax.rem(me - first + i, count))
            return carry

        lax.fori_loop(1, count, one, 0)

    other = me - 2 * upper - core + 2 - 2 * upper
    greet(start[0] + 1 - core)
    greet(other)
    greet(other + 1)
    greetings = jnp.int32(3)
    for level in range(LEVELS - 1, 0, -1):

        def greet_holder(head, count):
            target, _ = holder(level, head)

            @pl.when(target != me)
            def _():
                greet(target)

            return count + jnp.where(target != me, 1, 0)

        greetings = lax.fori_loop(0, HEADS, greet_holder, greetings)
    for level in (level4, level3):

        @pl.when(level > 0)
        def _():
            greet_members(4 << level)

        greetings = greetings + jnp.where(level > 0, lax.shift_left(4, jnp.maximum(level, 0)) - 1, 0)

    def load(head, carry):
        lanes = pl.ds(pl.multiple_of(head * DH, DH), DH)
        for pair, half, ref in ((0, 0, q_ref), (0, 1, g_ref), (1, 0, k_ref), (1, 1, v_ref)):
            pltpu.make_async_copy(
                ref.at[:, lanes], s0.at[head, pair, :, pl.ds(half * DH, DH)], load_sem
            ).start()
        return carry

    lax.fori_loop(0, HEADS, load, 0)

    row = lax.broadcasted_iota(jnp.int32, (TOKENS, TOKENS), 0)
    col = lax.broadcasted_iota(jnp.int32, (TOKENS, TOKENS), 1)
    upper8 = lax.broadcasted_iota(jnp.int32, (16, 256), 0) < 8
    arrived(s0, load_sem)

    def select(head, carry):
        pick = (position(row, off_ref, head) == col).astype(F32).astype(BF16)
        sel0 = nn(pick, s0[head, 0])
        sel1 = nn(pick, s0[head, 1])
        sbuf[head, 0] = sel0[:112].astype(BF16)
        sbuf[head, 1] = sel1[:112].astype(BF16)
        s4[head] = jnp.where(upper8, sel0[112:], sel1[112:]).astype(BF16)
        return carry

    lax.fori_loop(0, HEADS, select, 0)

    pl.semaphore_wait(barrier, greetings)

    def in_copy(level, head):
        rows = ROWS[level]
        target, slot = holder(level, head)
        if level == 0:
            src = s0.at[head]
            at = upper * HALF + core * TOKENS
        elif level < 4:
            src = sbuf.at[head, :, pl.ds(FIRST[level], rows), :]
            at = inside[level] * rows
        else:
            src = s4.at[head]
        if level < 4:
            dst = ubuf.at[slot, :, pl.ds(pl.multiple_of(at, rows), rows), :]
        else:
            dst = u4.at[me]
        return src, dst, target, in_send.at[level * HEADS + head], in_recv.at[slot]

    def kv_copy(head):
        target, slot = holder(0, head)
        at = pl.ds(pl.multiple_of(core * TOKENS, TOKENS), TOKENS)
        return s0.at[head, 1], ubuf.at[slot, 1, at, :], target + 2, kv_send.at[head], kv_recv.at[slot]

    turn = me
    for level in range(LEVELS - 1, -1, -1):

        def send_rows(i, carry):
            head = lax.rem(turn + i, HEADS)
            push(*in_copy(level, head))
            if level == 0:

                @pl.when(upper == 0)
                def _():
                    remote(*kv_copy(head))

            return carry

        lax.fori_loop(0, HEADS, send_rows, 0)

    key_i = lax.broadcasted_iota(jnp.int32, (HALF, HALF), 0)
    query_i = lax.broadcasted_iota(jnp.int32, (HALF, HALF), 1)
    causal = key_i <= query_i

    def does(level, j):
        return (level > 0) | ((level == 0) & (upper == j))

    def forward(step, carry):
        u = SLOTS - 1 - step
        level = level_of(u)
        head = head_of(u)

        @pl.when(level == 0)
        def _():
            arrived(ubuf.at[u, :, pl.ds(0, HALF), :], in_recv.at[u])

            @pl.when(upper == 1)
            def _():
                arrived(ubuf.at[u, 1, pl.ds(0, HALF), :], kv_recv.at[u])

        @pl.when((level > 0) & (level < 4))
        def _():
            arrived(ubuf.at[u], in_recv.at[u])

        @pl.when(level == 4)
        def _():
            arrived(u4, in_recv.at[u])

            def unpack(n, c):
                block = u4[pl.ds(n * 8, 8)].astype(F32)
                rows = pl.ds(pl.multiple_of(n * 64, 64), 64)
                ubuf[u, 0, rows, :] = block[:, :8, :].reshape(64, 256).astype(BF16)
                ubuf[u, 1, rows, :] = block[:, 8:, :].reshape(64, 256).astype(BF16)
                return c

            lax.fori_loop(0, 8, unpack, 0)

        for j in range(2):

            @pl.when(does(level, j))
            def _():
                keys = HALF * (j + 1)
                cols = pl.ds(j * HALF, HALF)
                q = ubuf[u, 0, cols, :DH]
                g = ubuf[u, 0, cols, DH:]
                k = ubuf[u, 1, :keys, :DH]
                v = ubuf[u, 1, :keys, DH:]
                s = nt(k, q) * SCALE
                last = jnp.where(causal, s[j * HALF :], MASKED)
                s = last if j == 0 else jnp.concatenate([s[:HALF], last], axis=0)
                m = jnp.max(s, axis=0, keepdims=True)
                e = jnp.exp(s - m)
                den = jnp.sum(e, axis=0, keepdims=True)
                ebuf[u, :keys, cols] = e
                abuf[u, :, cols] = tn(v, e.astype(BF16))
                dp = nt(v, g)
                dbuf[u, :keys, cols] = dp
                t = jnp.sum(e * dp, axis=0, keepdims=True)
                tile = jnp.concatenate([m, den, t, jnp.zeros((5, HALF), F32)], axis=0)
                stbuf[u, 2 * j] = tile[:, :128]
                stbuf[u, 2 * j + 1] = tile[:, 128:]

        @pl.when(level >= 0)
        def _():
            count = jnp.where(level == 0, 2, 4 << level)
            first = me - lax.rem(me, count)
            block = jnp.where(level == 0, 2 * upper, 0)

            def send_stats(i, c):
                push(
                    stbuf.at[u, block + lax.shift_right_logical(i, level)],
                    stin.at[level * HEADS + head],
                    first + i,
                    st_send.at[tiles_of(u) + i],
                    st_recv,
                )
                return c

            lax.fori_loop(0, count, send_stats, 0)

        return carry

    lax.fori_loop(0, SLOTS, forward, 0)

    arrived(stin, st_recv)
    lane = lax.broadcasted_iota(jnp.int32, (1, TOKENS), 1)
    spread = [None]
    stats = [stin[:HEADS]]
    for level in range(1, LEVELS):
        base = (inside[level] & ((1 << level) - 1)) * ROWS[level]
        rep = (row == base + lax.shift_right_logical(col, level)).astype(F32).astype(BF16)
        spread.append(rep)
        tiles = stin[level * HEADS : (level + 1) * HEADS].reshape(HEADS * 8, TOKENS)
        stats.append(move(tiles, rep, ((1,), (0,))).reshape(HEADS, 8, TOKENS))
    answers = [[] for _ in range(LEVELS)]
    for head in range(HEADS):
        chosen = [None] + [
            (lane & ((1 << level) - 1)) == off_ref[level, head] for level in range(1, LEVELS)
        ]
        ms = [stats[0][head, 0:1]] + [
            jnp.where(chosen[level], stats[level][head, 0:1], MASKED) for level in range(1, LEVELS)
        ]
        top = ms[0]
        for level in range(1, LEVELS):
            top = jnp.maximum(top, ms[level])
        total = jnp.zeros((1, TOKENS), F32)
        delta = jnp.zeros((1, TOKENS), F32)
        for level in range(LEVELS):
            weight = jnp.exp(ms[level] - top)
            den, t = stats[level][head, 1:2], stats[level][head, 2:3]
            if level:
                den = jnp.where(chosen[level], den, 0.0)
                t = jnp.where(chosen[level], t, 0.0)
            total = total + den * weight
            delta = delta + t * weight
        log_total = top + jnp.log(total)
        delta = delta * jnp.exp(top - log_total)
        lse_ref[head : head + 1, :] = log_total
        answer = jnp.concatenate([log_total, delta, jnp.zeros((6, TOKENS), F32)], axis=0)
        for level in range(LEVELS):
            answers[level].append(answer if level == 0 else jnp.where(chosen[level], answer, 0.0))

    def c_copy(level, head):
        n = level * HEADS + head
        target, slot = holder(level, head)
        return cout.at[n], cin.at[tiles_of(slot) + inside[level]], target, c_send.at[n], c_recv.at[slot]

    for level in range(LEVELS - 1, -1, -1):
        if level:
            packed = move(jnp.concatenate(answers[level], axis=0), spread[level], ((1,), (1,)))
            packed = packed.reshape(HEADS, 8, TOKENS)
        for head in range(HEADS):
            cout[level * HEADS + head] = packed[head] if level else answers[0][head]

        def send_answer(i, carry):
            push(*c_copy(level, lax.rem(turn + i, HEADS)))
            return carry

        lax.fori_loop(0, HEADS, send_answer, 0)

    def res_copy(u, level, i, head):
        rows = ROWS[level]
        if level < 4:
            at = i * rows if level else upper * HALF + i * rows
            src = obuf.at[u, :, pl.ds(pl.multiple_of(at, rows), rows), :]
        else:
            src = o4.at[i]
        if level == 0:
            dst, sem = r0.at[head], res_recv.at[0]
        elif level < 4:
            dst, sem = rbuf.at[head, :, pl.ds(FIRST[level], rows), :], res_recv.at[1]
        else:
            dst, sem = r4.at[head], res_recv.at[2]
        return src, dst, start[level] + i, res_send.at[tiles_of(u) + i], sem

    def res_kv_copy(u, i, head):
        src = obuf.at[u, 1, pl.ds(pl.multiple_of(i * TOKENS, TOKENS), TOKENS), :]
        return src, r0b.at[head], start[0] - 2 + i, res_kv_send.at[2 * u + i], res_recv.at[3]

    def backward(u, carry):
        level = level_of(u)
        head = head_of(u)
        base = tiles_of(u)
        for lv in range(LEVELS):

            @pl.when(level == lv)
            def _():
                arrived(cin.at[pl.ds(base, GROUP[lv])], c_recv.at[u])

        per = lax.shift_left(1, jnp.maximum(level, 0))
        origin = jnp.where(level == 0, base - 2 * upper, base)

        for j in range(2):

            @pl.when(does(level, j))
            def _():
                blocks = []
                for b in range(2 * j, 2 * j + 2):
                    blocks.append(
                        lax.fori_loop(
                            0, per, lambda i, c: c + cin[origin + b * per + i], jnp.zeros((8, TOKENS), F32)
                        )
                    )
                keys = HALF * (j + 1)
                cols = pl.ds(j * HALF, HALF)
                q = ubuf[u, 0, cols, :DH]
                g = ubuf[u, 0, cols, DH:]
                k = ubuf[u, 1, :keys, :DH]
                answer = jnp.concatenate(blocks, axis=1)
                m = jnp.concatenate([stbuf[u, 2 * j], stbuf[u, 2 * j + 1]], axis=1)[0:1]
                w = jnp.exp(m - answer[0:1])
                delta = answer[1:2]
                p = ebuf[u, :keys, cols] * w
                ds = (SCALE * p * (dbuf[u, :keys, cols] - delta)).astype(BF16)
                p = p.astype(BF16)
                o = (abuf[u, :, cols] * w).T
                dq = tn(k, ds).T
                obuf[u, 0, cols, :DH] = o.astype(BF16)
                obuf[u, 0, cols, DH:] = dq.astype(BF16)
                dk = nn(ds, q)
                dv = nn(p, g)
                if j == 0:
                    acc[:, :DH] = dk
                    acc[:, DH:] = dv
                    obuf[u, 1, :HALF, :DH] = dk.astype(BF16)
                    obuf[u, 1, :HALF, DH:] = dv.astype(BF16)
                else:
                    both = level > 0
                    obuf[u, 1, :HALF, :DH] = (dk[:HALF] + jnp.where(both, acc[:, :DH], 0.0)).astype(BF16)
                    obuf[u, 1, :HALF, DH:] = (dv[:HALF] + jnp.where(both, acc[:, DH:], 0.0)).astype(BF16)
                    obuf[u, 1, HALF:, :DH] = dk[HALF:].astype(BF16)
                    obuf[u, 1, HALF:, DH:] = dv[HALF:].astype(BF16)

        @pl.when(level == 4)
        def _():
            def pack(n, c):
                rows = pl.ds(pl.multiple_of(n * 64, 64), 64)
                lo = obuf[u, 0, rows, :].astype(F32).reshape(8, 8, 256)
                hi = obuf[u, 1, rows, :].astype(F32).reshape(8, 8, 256)
                o4[pl.ds(n * 8, 8)] = jnp.concatenate([lo, hi], axis=1).astype(BF16)
                return c

            lax.fori_loop(0, 8, pack, 0)

        for lv in range(LEVELS):

            @pl.when(level == lv)
            def _():
                def send_result(i, c):
                    push(*res_copy(u, lv, lax.rem(i + turn, GROUP[lv]), head))
                    if lv == 0:

                        @pl.when(upper == 1)
                        def _():
                            remote(*res_kv_copy(u, i, head))

                    return c

                lax.fori_loop(0, GROUP[lv], send_result, 0)

        return carry

    lax.fori_loop(0, SLOTS, backward, 0)

    def drain_own(head, carry):
        for level in range(LEVELS):
            src, _, target, sem, _ = in_copy(level, head)
            sent(src, target, sem)
            src, _, target, sem, _ = c_copy(level, head)
            sent(src, target, sem)

        @pl.when(upper == 0)
        def _():
            src, _, _, sem, _ = kv_copy(head)
            done(src, sem)

        return carry

    lax.fori_loop(0, HEADS, drain_own, 0)

    def drain(u, carry):
        level = level_of(u)
        for lv in range(LEVELS):

            @pl.when(level == lv)
            def _():
                def one(i, c):
                    src, _, target, sem, _ = res_copy(u, lv, i, 0)
                    sent(src, target, sem)
                    sent(stbuf.at[u, 0], target, st_send.at[tiles_of(u) + i])
                    if lv == 0:

                        @pl.when(upper == 1)
                        def _():
                            src, _, _, sem, _ = res_kv_copy(u, i, 0)
                            done(src, sem)

                    return c

                lax.fori_loop(0, GROUP[lv], one, 0)

        return carry

    lax.fori_loop(0, SLOTS, drain, 0)

    arrived(r4, res_recv.at[2])
    arrived(rbuf, res_recv.at[1])
    arrived(r0, res_recv.at[0])

    @pl.when(upper == 0)
    def _():
        arrived(r0b, res_recv.at[3])


def finish(off_ref, lse_ref, r0, r0b, rbuf, r4, out_ref, log_ref, dq_ref, dk_ref, dv_ref, w0, w0b, wbuf, res, log, in_sem, out_sem):
    upper = lax.rem(lax.div(lax.axis_index("seq"), 2), 2)
    row = lax.broadcasted_iota(jnp.int32, (TOKENS, TOKENS), 0)
    col = lax.broadcasted_iota(jnp.int32, (TOKENS, TOKENS), 1)

    def ins(head):
        return (
            pltpu.make_async_copy(r0.at[head], w0.at[head], in_sem.at[0, head]),
            pltpu.make_async_copy(r0b.at[head], w0b.at[head], in_sem.at[1, head]),
            pltpu.make_async_copy(rbuf.at[head], wbuf.at[head, :, pl.ds(0, 112), :], in_sem.at[2, head]),
            pltpu.make_async_copy(r4.at[head], wbuf.at[head, 0, pl.ds(112, 16), :], in_sem.at[3, head]),
            pltpu.make_async_copy(r4.at[head], wbuf.at[head, 1, pl.ds(112, 16), :], in_sem.at[4, head]),
        )

    def outs(head):
        lanes = pl.ds(head * DH, DH)
        return [
            pltpu.make_async_copy(res.at[n, head], ref.at[:, lanes], out_sem.at[n, head])
            for n, ref in enumerate((out_ref, dq_ref, dk_ref, dv_ref))
        ]

    for head in range(HEADS):
        for copy in ins(head):
            copy.start()
    log_in = pltpu.make_async_copy(lse_ref, log, in_sem.at[5, 0])
    log_out = pltpu.make_async_copy(log, log_ref, out_sem.at[4, 0])
    log_in.start()
    puts = []
    for head in range(HEADS):
        hit = position(col, off_ref, head) == row
        puts.append((
            (hit & (col < 120)).astype(F32).astype(BF16),
            (hit & ((col < 112) | (col >= 120))).astype(F32).astype(BF16),
        ))
    log_in.wait()
    log_out.start()
    for head in range(HEADS):
        for copy in ins(head):
            copy.wait()
        all0 = w0[head, 0].astype(F32) + nn(puts[head][0], wbuf[head, 0])
        all1 = w0[head, 1].astype(F32) + nn(puts[head][1], wbuf[head, 1])
        all1 = all1 + jnp.where(upper == 0, w0b[head].astype(F32), 0.0)
        res[0, head] = all0[:, :DH].astype(BF16)
        res[1, head] = all0[:, DH:].astype(BF16)
        res[2, head] = all1[:, :DH].astype(BF16)
        res[3, head] = all1[:, DH:].astype(BF16)
        for copy in outs(head):
            copy.start()
    for head in range(HEADS):
        for copy in outs(head):
            copy.wait()
    log_out.wait()


def on_device(query_in, key_in, value_in, grad_out, offsets):
    hbm = pl.BlockSpec(memory_space=pl.ANY)
    smem = pl.BlockSpec(memory_space=pltpu.SMEM)
    parts = pl.pallas_call(
        kernel,
        out_shape=(
            jax.ShapeDtypeStruct((HEADS, TOKENS), F32),
            jax.ShapeDtypeStruct((HEADS, 2, TOKENS, 256), BF16),
            jax.ShapeDtypeStruct((HEADS, TOKENS, 256), BF16),
            jax.ShapeDtypeStruct((HEADS, 2, 112, 256), BF16),
            jax.ShapeDtypeStruct((HEADS, 16, 256), BF16),
        ),
        in_specs=[hbm] * 4 + [smem],
        out_specs=(pl.BlockSpec(memory_space=pltpu.VMEM),) + (hbm,) * 4,
        scratch_shapes=[
            pltpu.VMEM((HEADS, 2, TOKENS, 256), BF16),
            pltpu.VMEM((HEADS, 2, 112, 256), BF16),
            pltpu.VMEM((HEADS, 16, 256), BF16),
            pltpu.VMEM((SLOTS, 2, SUB, 256), BF16),
            pltpu.VMEM((SEQ_DEVICES, 16, 256), BF16),
            pltpu.VMEM((SLOTS, SUB, SUB), F32),
            pltpu.VMEM((SLOTS, SUB, SUB), F32),
            pltpu.VMEM((SLOTS, DH, SUB), F32),
            pltpu.VMEM((SLOTS, 4, 8, 128), F32),
            pltpu.VMEM((LEVELS * HEADS, 8, 128), F32),
            pltpu.VMEM((LEVELS * HEADS, 8, 128), F32),
            pltpu.VMEM((TILES, 8, 128), F32),
            pltpu.VMEM((HALF, 256), F32),
            pltpu.VMEM((SLOTS, 2, SUB, 256), BF16),
            pltpu.VMEM((SEQ_DEVICES, 16, 256), BF16),
            pltpu.SemaphoreType.DMA,
            pltpu.SemaphoreType.DMA((LEVELS * HEADS,)),
            pltpu.SemaphoreType.DMA((HEADS,)),
            pltpu.SemaphoreType.DMA((SLOTS,)),
            pltpu.SemaphoreType.DMA((3,)),
            pltpu.SemaphoreType.DMA((TILES,)),
            pltpu.SemaphoreType.DMA,
            pltpu.SemaphoreType.DMA((LEVELS * HEADS,)),
            pltpu.SemaphoreType.DMA((SLOTS,)),
            pltpu.SemaphoreType.DMA((TILES,)),
            pltpu.SemaphoreType.DMA((6,)),
            pltpu.SemaphoreType.DMA((4,)),
        ],
        compiler_params=pltpu.CompilerParams(
            collective_id=0, has_side_effects=True, vmem_limit_bytes=60 * 1024 * 1024
        ),
    )(query_in, key_in, value_in, grad_out, offsets)
    flat = jax.ShapeDtypeStruct((TOKENS, HEADS * DH), BF16)
    return pl.pallas_call(
        finish,
        out_shape=(flat, jax.ShapeDtypeStruct((HEADS, TOKENS), F32), flat, flat, flat),
        in_specs=[smem] + [hbm] * 5,
        out_specs=(hbm,) * 5,
        scratch_shapes=[
            pltpu.VMEM((HEADS, 2, TOKENS, 256), BF16),
            pltpu.VMEM((HEADS, TOKENS, 256), BF16),
            pltpu.VMEM((HEADS, 2, TOKENS, 256), BF16),
            pltpu.VMEM((4, HEADS, TOKENS, DH), BF16),
            pltpu.VMEM((HEADS, TOKENS), F32),
            pltpu.SemaphoreType.DMA((6, HEADS)),
            pltpu.SemaphoreType.DMA((5, HEADS)),
        ],
        compiler_params=pltpu.CompilerParams(vmem_limit_bytes=60 * 1024 * 1024),
    )(offsets, *parts)


def solution(mesh):
    return jax.shard_map(
        on_device,
        mesh=mesh,
        in_specs=(P("seq", "head"),) * 4 + (P(None, "head"),),
        out_specs=(P("seq", "head"), P("head", "seq")) + (P("seq", "head"),) * 3,
        check_vma=False,
    )
```
